32 devices in a mesh: groups: 1, dp: 32 (over z, y, x, core).
Axes of the slice: x: 2, y: 2, z: 4, core: 2. Of those that a mesh axis runs over, the one named last changes fastest.
Arguments:
- learn_hidden: bfloat16 [4096, 1536], P(('groups', 'dp')), may hold values from -6 to 6
- learn_cotangent: bfloat16 [4096, 2048], P(('groups', 'dp')), may hold values from -0.1875 to 0.1875
- master: float32 [192, 128, 128], P('dp'), may hold values from -0.15625 to 0.15625
- moment_first: float32 [192, 128, 128], P('dp'), may hold values from -0.18 to 0.18
- moment_second: float32 [192, 128, 128], P('dp'), may hold values from 0.01 to 0.2
- resident_weight: bfloat16 [24576, 2048], P('dp'), may hold values from -440 to 440
- resident_scale: float32 [192, 16], P('dp'), may hold values from 0.0001 to 0.0006
- placement: int32 [16], replicated, may hold values from 0 to 15, each once
- decode_hidden: bfloat16 [4, 256, 8, 1536], P(None, ('groups', 'dp')), may hold values from -6 to 6
- routing: int32 [4, 256, 8], P(None, ('groups', 'dp')), may hold values from 0 to 15, all different within a row; in each aligned block of 8 rows (0 to 7, 8 to 15, ..., all dimensions but the last counted through in order) at most 6 rows name the same one
- gate_weight: float32 [4, 256, 8], P(None, ('groups', 'dp')), may hold values from 0.05 to 1
Outputs:
- decoded: bfloat16 [4, 256, 2048], P(None, ('groups', 'dp'))
- new_master: float32 [192, 128, 128], P(('groups', 'dp'))
The draws below stay inside these ranges and needn't reach their ends.
Inputs may be any that keep to these rules, and one draw needn't show every extreme that they name: `routing`: in every decode step, the 8 rows of one device name each expert at most 6 times, a bound that some block reaches; a row names 8 different experts. `placement`: each owner pair serves exactly one expert.
All inputs are finite; a program needn't handle non-finite values.
Results may differ from the reference program's by a relative error of at most 0.009.
Values may be sent and summed in bfloat16 or wider, within the bound.
No kernel may reach another device: no remote copies, remote signals or barrier semaphores. Data moves between devices by JAX's collectives and lax.ppermute only.
A program may use at most 128 MiB of HBM per device.

```python
import math
import jax
import jax.numpy as jnp
import numpy as np
from jax import lax

D = 2048
HID = 1536
BLK = 128
TOPK = 8
STEPS = 4
DEC_DEV = 8
EXPERTS = 16
CAP = 6
BLOCKS = 192
LEARN_TOKENS = 4096
DEC_ROWS = 256
N_DP = 32


def with_spikes(values, rng, source, target, parts, factor):
    def block_of(axis_at):
        return (jnp.arange(values.shape[axis_at]) // (values.shape[axis_at] // parts)).reshape((-1,) + (1,) * (values.ndim - 1 - axis_at))

    one_side = jax.random.permutation(rng, parts)[block_of(target)]
    far = (block_of(target) + parts // 2) % parts
    return jnp.where((block_of(source) == one_side) | (block_of(source) == far), factor * values, values)


def shard_levels(key, shape, cuts, low, high):
    gain, own = 1.0, jax.random.fold_in(key, 6)
    for axis_at, parts in cuts:
        draws = jnp.exp(jax.random.uniform(jax.random.fold_in(own, axis_at), (parts,), jnp.float32, low / len(cuts), high / len(cuts)))
        gain = gain * jnp.repeat(draws, shape[axis_at] // parts).reshape([-1 if axis == axis_at else 1 for axis in range(len(shape))])
    return gain


def assign_block(own_key, own, number, rows, number_of, top, most, lean):
    sequence = jax.random.permutation(own_key, number_of)
    packed, usual = portions_of(number_of, rows * top, most, lean, True), portions_of(number_of, rows * top, most, lean, False)
    places = jnp.arange(number_of)

    def named(tallies, turn):
        used = int((tallies > 0).sum())
        fixed = max(1, used // 4)
        passed = fixed + (places - fixed + turn * (used - fixed)) % max(1, number_of - fixed)
        return jnp.zeros((number_of,), jnp.int32).at[sequence[jnp.where(places < fixed, places, passed)]].set(jnp.asarray(tallies, jnp.int32))

    tallies = jnp.where(number % 4 == 0, named(packed, number // 4), named(usual, number - number // 4 - 1))
    mixed = jax.random.permutation(jax.random.fold_in(own, 3), number_of)
    donor, receiver = mixed[0:number_of // 2 * 2:2], mixed[1:number_of // 2 * 2:2]
    margin = jnp.minimum(tallies[donor] - 1, most - tallies[receiver]) // 2
    margin = jnp.where((donor == sequence[0]) | (receiver == sequence[0]) | (tallies[receiver] == 0), 0, jnp.maximum(margin, 0))
    passed = jax.random.randint(jax.random.fold_in(own, 4), (number_of // 2,), 0, 1 << 20) % (margin + 1)
    tallies = tallies.at[donor].add(-passed).at[receiver].add(passed)
    items = jnp.searchsorted(jnp.cumsum(tallies), jnp.arange(rows * top), side="right").astype(jnp.int32)
    grid = items.reshape(top, rows).T
    grid = grid[jax.random.permutation(jax.random.fold_in(own, 1), rows)]
    turn = jax.random.randint(jax.random.fold_in(own, 2), (rows, 1), 0, top)
    return jnp.take_along_axis(grid, (jnp.arange(top)[None, :] + turn) % top, axis=1)


def portions_of(count, total, bound, slope, full):
    portions = [(1 << 20) // math.isqrt(grade ** slope) + 1 for grade in range(1, count + 1)]
    largest = bound if full else min(bound, max(-(-total // count), total * portions[0] // sum(portions)))
    least = 1 if total - largest >= count - 1 else 0
    holding, spare = [largest] + [least] * (count - 1), total - largest - least * (count - 1)
    while spare > 0:
        free = [i for i in range(1, count) if holding[i] < largest] or [i for i in range(1, count) if holding[i] < bound]
        mass, left = sum([portions[i] for i in free]), spare
        for i in free:
            extra = min(bound - holding[i], max(1, left * portions[i] // mass), spare)
            holding[i] = holding[i] + extra
            spare = spare - extra
    return np.array(holding)


def scatter_about(own_key, extent, width, reach, pieces=(), held_as=jnp.bfloat16):
    array = width * jax.random.normal(own_key, extent, jnp.float32)
    if pieces:
        array = array * shard_levels(own_key, extent, pieces, -0.22, 0.18)
    return jnp.clip(array, -reach, reach).astype(held_as)


def heavy_noise(own_key, extent, scale, most, shards, heavy, kind=jnp.bfloat16):
    result = scale * jax.random.normal(own_key, extent, jnp.float32)
    if shards:
        result = result * shard_levels(own_key, extent, shards, -0.22, 0.18)
    return jnp.clip(with_spikes(result, jax.random.fold_in(own_key, 3), *heavy), -most, most).astype(kind)


def setup_inputs(seed: int = 0, part: int = 0) -> dict:
    seeds = jax.random.split(jax.random.key(seed), 12)
    part_splits = jax.random.split(jax.random.fold_in(seeds[11], part), 12)
    learn_hidden = scatter_about(part_splits[0], (LEARN_TOKENS, HID), 1.0, 6.0, ((0, 32),))
    learn_cotangent = heavy_noise(part_splits[1], (LEARN_TOKENS, D), LEARN_TOKENS ** -0.5, 0.1875, ((0, 32),), (0, 1, 32, 2.75))
    master = scatter_about(seeds[2], (BLOCKS, BLK, BLK), HID ** -0.5, 0.15625, ((0, 32),), jnp.float32)
    moment_first = scatter_about(seeds[3], (BLOCKS, BLK, BLK), 0.03, 0.18, ((0, 32),), jnp.float32)
    moment_second = jnp.clip(jnp.exp(math.log(0.2) - 2.9957323 * jax.random.uniform(seeds[4], (BLOCKS, BLK, BLK), jnp.float32) ** shard_levels(seeds[4], (BLOCKS, BLK, BLK), ((0, 32),), -0.2, 0.2)), 0.01, 0.2)
    resident_weight = scatter_about(seeds[5], (EXPERTS * HID, D), 100.0, 440.0, ((0, 32),))
    resident_scale = jnp.clip(jnp.exp(math.log(0.0006) - 1.7917595 * jax.random.uniform(seeds[6], (EXPERTS * HID // BLK, D // BLK), jnp.float32) ** shard_levels(seeds[6], (EXPERTS * HID // BLK, D // BLK), ((0, 32),), -0.2, 0.2)), 0.0001, 0.0006)
    placement = jax.random.permutation(seeds[7], EXPERTS).astype(jnp.int32)
    decode_hidden = scatter_about(part_splits[8], (STEPS, DEC_ROWS, TOPK, HID), 1.0, 6.0, ((1, 32),))
    routing_keys = jax.random.split(jax.random.fold_in(part_splits[9], 1), STEPS * DEC_ROWS // DEC_DEV)
    routing_turns = jax.random.permutation(jax.random.fold_in(part_splits[9], 3), STEPS * DEC_ROWS // DEC_DEV)
    routing = jax.vmap(lambda own, number: assign_block(jax.random.fold_in(part_splits[9], 2), own, number, DEC_DEV, EXPERTS, TOPK, CAP, 2))(routing_keys, routing_turns).reshape((STEPS, DEC_ROWS, TOPK))
    gate_weight = jnp.clip(0.05 + 0.95 * jax.random.uniform(part_splits[10], (STEPS, DEC_ROWS, TOPK), jnp.float32) ** shard_levels(part_splits[10], (STEPS, DEC_ROWS, TOPK), ((1, 32),), -0.2, 0.2), 0.05, 1.0)
    return dict(learn_hidden=learn_hidden, learn_cotangent=learn_cotangent, master=master, moment_first=moment_first, moment_second=moment_second, resident_weight=resident_weight, resident_scale=resident_scale, placement=placement, decode_hidden=decode_hidden, routing=routing, gate_weight=gate_weight)


learn_rate = 0.05
beta_first = 0.9
beta_second = 0.95
correct_first = 1.0 - 0.9 ** 10
correct_second = 1.0 - 0.95 ** 10
decay_rate = 0.1
adam_epsilon = 1e-08
quant_range = 448.0

def optimizer(gradient, master, moment_first, moment_second):
    first_moment = beta_first * moment_first + (1.0 - beta_first) * gradient
    second_moment = beta_second * moment_second + (1.0 - beta_second) * gradient * gradient
    update = first_moment / correct_first / (jnp.sqrt(second_moment / correct_second) + adam_epsilon)
    return master - learn_rate * (update + decay_rate * master)

def quantize(weights):
    largest = lax.optimization_barrier(jnp.max(jnp.abs(weights), axis=(1, 2)))
    scales = (largest + 1e-06) / quant_range
    quantized = (weights / scales[:, None, None]).astype(jnp.bfloat16)
    return (quantized, scales)

def half_partial(input_rows, weights, scales, begin_block, end_block):
    summed = jnp.zeros((input_rows.shape[0], D // BLK, BLK), jnp.float32)
    for row_block in range(begin_block, end_block):
        product = jnp.dot(input_rows[:, row_block * BLK:(row_block + 1) * BLK], weights[row_block * BLK:(row_block + 1) * BLK], preferred_element_type=jnp.float32)
        summed = summed + product.reshape(input_rows.shape[0], D // BLK, BLK) * scales[row_block][:, None]
    return summed.reshape(input_rows.shape[0], D).astype(jnp.bfloat16)

def reference(learn_hidden, learn_cotangent, master, moment_first, moment_second, resident_weight, resident_scale, placement, decode_hidden, routing, gate_weight):
    gradient = jnp.dot(learn_hidden.T, learn_cotangent, preferred_element_type=jnp.float32)
    gradient = gradient.reshape(HID // BLK, BLK, D // BLK, BLK).transpose(0, 2, 1, 3).reshape(BLOCKS, BLK, BLK)
    new_master = optimizer(gradient, master, moment_first, moment_second)
    quantized, scales = quantize(new_master)
    fresh_weight = quantized.reshape(HID // BLK, D // BLK, BLK, BLK).transpose(0, 2, 1, 3).reshape(HID, D)
    fresh_scale = scales.reshape(HID // BLK, D // BLK)
    routed = routing.reshape(-1)
    hidden_rows = decode_hidden.reshape(-1, HID)
    gate_values = gate_weight.reshape(-1)
    counts = lax.optimization_barrier(jnp.sum((routed[None, :] == jnp.arange(EXPERTS, dtype=jnp.int32)[:, None]).astype(jnp.int32), axis=1))
    offsets = (jnp.cumsum(counts) - counts).astype(jnp.int32)
    longest = STEPS * N_DP * CAP
    sorted_entries = jnp.argsort(routed, stable=True).astype(jnp.int32)
    sorted_entries = jnp.concatenate([sorted_entries, jnp.zeros((longest,), jnp.int32)])
    row_blocks = HID // BLK

    def one_expert(outputs, expert):
        chosen = lax.dynamic_slice_in_dim(sorted_entries, offsets[expert], longest)
        live_mask = (jnp.arange(longest, dtype=jnp.int32) < counts[expert]).astype(jnp.float32)
        owner_pair = placement[expert].astype(jnp.int32)
        weights = jnp.where(expert == 0, fresh_weight, lax.dynamic_slice_in_dim(resident_weight, owner_pair * HID, HID, 0))
        scale_table = jnp.where(expert == 0, fresh_scale, lax.dynamic_slice_in_dim(resident_scale, owner_pair * row_blocks, row_blocks, 0))
        gathered_rows = hidden_rows[chosen]
        first_half = half_partial(gathered_rows, weights, scale_table, 0, row_blocks // 2)
        second_half = half_partial(gathered_rows, weights, scale_table, row_blocks // 2, row_blocks)
        expert_out = (first_half.astype(jnp.float32) + second_half.astype(jnp.float32)).astype(jnp.bfloat16)
        expert_out = lax.optimization_barrier(expert_out)
        values = expert_out.astype(jnp.float32) * (gate_values[chosen] * live_mask)[:, None]
        return (outputs.at[chosen // TOPK].add(values), None)
    outputs = jnp.zeros((STEPS * DEC_ROWS, D), jnp.float32)
    outputs, _ = lax.scan(one_expert, outputs, jnp.arange(EXPERTS, dtype=jnp.int32))
    return (outputs.astype(jnp.bfloat16).reshape(STEPS, DEC_ROWS, D), new_master)
```

```python
import jax
import jax.numpy as jnp
from jax import lax
from jax.experimental import pallas as pl
from jax.experimental.pallas import tpu as pltpu
from jax.sharding import PartitionSpec as P

learn_rate = 0.05
beta_first = 0.9
beta_second = 0.95
correct_first = 1.0 - 0.9**10
correct_second = 1.0 - 0.95**10
decay_rate = 0.1
adam_epsilon = 1e-08
quant_range = 448.0

F32 = jnp.float32
BF16 = jnp.bfloat16
PARAMS = pltpu.CompilerParams(vmem_limit_bytes=40 * 2**20)


def optimizer(gradient, master, moment_first, moment_second):
    first_moment = beta_first * moment_first + (1.0 - beta_first) * gradient
    second_moment = beta_second * moment_second + (1.0 - beta_second) * gradient * gradient
    update = (
        first_moment / correct_first / (jnp.sqrt(second_moment / correct_second) + adam_epsilon)
    )
    return master - learn_rate * (update + decay_rate * master)


def quantize(weights):
    largest = jnp.max(jnp.abs(weights), axis=(1, 2))
    scales = (largest + 1e-06) / quant_range
    quantized = (weights / scales[:, None, None]).astype(BF16)
    return (quantized, scales)


def vmem(count):
    return [pl.BlockSpec(memory_space=pltpu.VMEM)] * count


def pack_kernel(
    steps,
    experts,
    capacity,
    placement,
    route_row,
    route_column,
    gate_row,
    hidden,
    packed,
    gates,
    gates_trained,
):
    entries = route_row.shape[1]
    step_entries = entries // steps
    topk = step_entries // (gates.shape[0] // 2 // steps)
    rows = gates.shape[0] // 2
    routed = route_row[...]
    lane = lax.broadcasted_iota(jnp.int32, (entries, entries), 1)
    line = lax.broadcasted_iota(jnp.int32, (entries, entries), 0)
    earlier = (lane // step_entries == line // step_entries) & (line // topk < lane // topk)
    same = (route_column[...] == routed) & earlier
    place = jnp.sum(jnp.where(same, 1.0, 0.0), axis=0, keepdims=True).astype(jnp.int32)
    pair = jnp.zeros_like(routed)
    for expert in range(experts):
        pair = jnp.where(routed == expert, placement[expert], pair)
    entry = lax.broadcasted_iota(jnp.int32, (1, entries), 1)
    step_slot = entry // step_entries * capacity + place
    slot = pair * (steps * capacity) + step_slot
    slots = gates.shape[1]
    onehot = jnp.where(
        lax.broadcasted_iota(jnp.int32, (slots, entries), 0) == slot, 1.0, 0.0
    ).astype(BF16)
    half = packed.shape[2]
    for side in range(2):
        packed[side] = jnp.dot(
            onehot, hidden[:, side * half : (side + 1) * half], preferred_element_type=F32
        ).astype(BF16)
    row = lax.broadcasted_iota(jnp.int32, (rows, entries), 0)
    mine = lax.broadcasted_iota(jnp.int32, (rows, entries), 1) // topk == row
    trained = routed == 0
    onehot_trained = jnp.where(
        (lax.broadcasted_iota(jnp.int32, (steps * capacity, entries), 0) == step_slot) & trained,
        1.0,
        0.0,
    ).astype(BF16)
    weight = jnp.where(mine, gate_row[...], 0.0)
    high = weight.astype(BF16)
    rest = (weight - high.astype(F32)).astype(BF16)
    plain = jnp.where(trained, 0.0, 1.0).astype(BF16)
    over_entries = (((1,), (1,)), ((), ()))
    for index, part in enumerate((high, rest)):
        at = slice(index * rows, (index + 1) * rows)
        gates[at] = lax.dot_general(
            part * plain, onehot, over_entries, preferred_element_type=F32
        ).astype(BF16)
        gates_trained[at] = lax.dot_general(
            part, onehot_trained, over_entries, preferred_element_type=F32
        ).astype(BF16)


def gradient_kernel(
    device_ref,
    hidden_own,
    hidden_other,
    cotangent_own,
    cotangent_other,
    first_sent,
    first_kept,
    second_sent,
    second_kept,
    hidden_across,
    cotangent,
):
    device = device_ref[0]
    tokens = hidden_own.shape[0]
    hidden_across[:, :tokens] = hidden_own[...].T
    hidden_across[:, tokens:] = hidden_other[...].T
    cotangent[:tokens] = cotangent_own[...]
    cotangent[tokens:] = cotangent_other[...]
    highs, _, blocks, side, _ = first_sent.shape
    column_blocks = cotangent.shape[1] // side
    wide = 2 if blocks % 2 == 0 else 1
    core = device % 2
    bit_x = device // 2 % 2
    bit_y = device // 4 % 2

    def fill(out, dest_of):
        def body(index, carry):
            high, free = index // 2, index % 2
            dest = dest_of(high, free)
            for at in range(0, blocks, wide):
                block = dest * blocks + at
                row = pl.multiple_of(block // column_blocks * side, side)
                column = pl.multiple_of(block % column_blocks * side, side)
                product = jnp.dot(
                    hidden_across[pl.ds(row, side), :],
                    cotangent[:, pl.ds(column, wide * side)],
                    preferred_element_type=F32,
                ).astype(out.dtype)
                for part in range(wide):
                    out[high, free, at + part] = product[:, part * side : (part + 1) * side]
            return carry

        lax.fori_loop(0, 2 * highs, body, 0)

    def number(high, y, x):
        return ((high * 2 + y) * 2 + x) * 2 + core

    fill(first_sent, lambda high, free: number(high, free, 1 - bit_x))
    fill(second_sent, lambda high, free: number(high + highs, 1 - bit_y, free))
    fill(first_kept, lambda high, free: number(high, free, bit_x))
    fill(second_kept, lambda high, free: number(high + highs, bit_y, free))


def trained_kernel(device_ref, plane, flips, rows, weights, out):
    device = device_ref[0]
    depth, blocks, side, _ = weights.shape
    inner = device % plane
    floor = device // plane
    column_blocks = plane * blocks
    for at in range(blocks):
        total = jnp.zeros((rows.shape[1], side), F32)
        for slot in range(depth):
            block = ((floor ^ flips[slot]) * plane + inner) * blocks + at
            row_block = block // out_columns(rows, plane, blocks, depth)
            total = total + jnp.dot(rows[row_block], weights[slot, at], preferred_element_type=F32)
        out[:, at * side : (at + 1) * side] = total.astype(out.dtype)


def out_columns(rows, plane, blocks, depth):
    return plane * blocks * depth // rows.shape[0]


def combine_kernel(returned, trained, gates, gates_trained, out):
    peers, _, width = trained.shape
    columns = out.shape[1]
    side = 128
    per_peer = width // side
    count = out.shape[0]
    for column in range(columns // side):
        at = slice(column * side, (column + 1) * side)
        fresh = None
        for number in range(column, peers * per_peer, columns // side):
            peer, block = divmod(number, per_peer)
            part = trained[peer, :, block * side : (block + 1) * side].astype(F32)
            fresh = part if fresh is None else fresh + part
        both = jnp.dot(gates[...], returned[:, at], preferred_element_type=F32) + jnp.dot(
            gates_trained[...], fresh.astype(BF16), preferred_element_type=F32
        )
        out[:, at] = (both[:count] + both[count:]).astype(out.dtype)


def local(
    learn_hidden,
    learn_cotangent,
    master,
    moment_first,
    moment_second,
    resident_weight,
    resident_scale,
    placement,
    decode_hidden,
    routing,
    gate_weight,
):
    devices = lax.axis_size("dp")
    device = lax.axis_index("dp")
    device_ref = device.astype(jnp.int32).reshape(1)
    blocks, side = master.shape[:2]
    hidden_width = learn_hidden.shape[1]
    columns = learn_cotangent.shape[1]
    row_blocks = hidden_width // side
    column_blocks = columns // side
    tokens = learn_hidden.shape[0]
    steps, step_rows, topk = routing.shape
    experts = placement.shape[0]
    capacity = min(step_rows, step_rows * topk // experts + 2)
    entries = steps * step_rows * topk
    pair_slots = steps * capacity
    slots = experts * pair_slots
    half = hidden_width // 2

    def flip(array, mask):
        return lax.ppermute(array, "dp", [(i, i ^ mask) for i in range(devices)])

    def bit(number):
        return device // 2**number % 2

    def pick(array, index, axis):
        return lax.dynamic_index_in_dim(array, index, axis, keepdims=False)

    routed = routing.reshape(1, entries)
    packed, gates, gates_trained = pl.pallas_call(
        lambda *refs: pack_kernel(steps, experts, capacity, *refs),
        out_shape=(
            jax.ShapeDtypeStruct((2, slots, half), BF16),
            jax.ShapeDtypeStruct((2 * steps * step_rows, slots), BF16),
            jax.ShapeDtypeStruct((2 * steps * step_rows, pair_slots), BF16),
        ),
        in_specs=[pl.BlockSpec(memory_space=pltpu.SMEM)] + vmem(4),
        out_specs=tuple(vmem(3)),
        compiler_params=PARAMS,
    )(
        placement,
        routed,
        routed.reshape(entries, 1),
        gate_weight.reshape(1, entries),
        decode_hidden.reshape(entries, hidden_width),
    )
    by_core = [list(range(0, devices, 2)) + list(range(1, devices, 2))]
    received = lax.all_to_all(
        packed.reshape(devices, pair_slots, half),
        "dp",
        split_axis=0,
        concat_axis=0,
        tiled=True,
        axis_index_groups=by_core,
    ).reshape(2, slots, half)

    highs = devices // 16
    part = jax.ShapeDtypeStruct((highs, 2, blocks, side, side), BF16)
    first_sent, first_kept, second_sent, second_kept = pl.pallas_call(
        gradient_kernel,
        out_shape=(part,) * 4,
        in_specs=[pl.BlockSpec(memory_space=pltpu.SMEM)] + vmem(4),
        out_specs=tuple(vmem(4)),
        scratch_shapes=[
            pltpu.VMEM((hidden_width, 2 * tokens), BF16),
            pltpu.VMEM((2 * tokens, columns), BF16),
        ],
        compiler_params=PARAMS,
    )(
        device_ref,
        learn_hidden,
        flip(learn_hidden, 1),
        learn_cotangent,
        flip(learn_cotangent, 1),
    )

    def halve(kept, arrived, number):
        total = kept.astype(F32) + arrived.astype(F32)
        return pick(total, 1 - bit(number), 1).astype(BF16), pick(total, bit(number), 1)

    first_sent, first_kept = halve(first_kept, flip(first_sent, 2), 2)
    second_sent, second_kept = halve(second_kept, flip(second_sent, 4), 1)
    first = first_kept + flip(first_sent, 4).astype(F32)
    second = second_kept + flip(second_sent, 2).astype(F32)
    gradient = jnp.concatenate([first, second], axis=0)
    number = 3
    while gradient.shape[0] > 1:
        split = gradient.reshape((-1, 2) + gradient.shape[1:])
        sent = pick(split, 1 - bit(number), 1).astype(BF16)
        gradient = pick(split, bit(number), 1) + flip(sent, 2**number).astype(F32)
        number += 1
    new_master = optimizer(gradient[0], master, moment_first, moment_second)
    quantized, scales = quantize(new_master)
    fresh = (quantized.astype(F32) * scales[:, None, None]).astype(BF16)

    scale_rows = jnp.repeat(resident_scale, side, axis=1)[:, None, :]
    weights = (
        (resident_weight.reshape(row_blocks // 2, side, columns).astype(F32) * scale_rows)
        .astype(BF16)
        .reshape(half, columns)
    )
    core = bit(0)
    sent = jnp.dot(pick(received, 1 - core, 0), weights, preferred_element_type=F32).astype(BF16)
    kept = jnp.dot(pick(received, core, 0), weights, preferred_element_type=F32).astype(BF16)
    expert_out = (kept.astype(F32) + flip(sent, 1).astype(F32)).astype(BF16)
    same_core = [list(range(0, devices, 2)), list(range(1, devices, 2))]
    returned = lax.all_to_all(
        expert_out.reshape(experts, pair_slots, columns),
        "dp",
        split_axis=0,
        concat_axis=0,
        tiled=True,
        axis_index_groups=same_core,
    ).reshape(slots, columns)

    plane = 1
    while plane * blocks % column_blocks:
        plane *= 2
    depth = devices // plane
    gathered = pick(packed.reshape(2, experts, pair_slots, half), placement[0], 1)[None]
    mask = 1
    while mask < plane:
        other = flip(gathered, mask)
        upper = device // mask % 2 == 1
        gathered = jnp.concatenate(
            [jnp.where(upper, other, gathered), jnp.where(upper, gathered, other)], axis=0
        )
        mask *= 2
    rows = (
        gathered.reshape(plane, 2, pair_slots, row_blocks // 2, side)
        .transpose(1, 3, 0, 2, 4)
        .reshape(row_blocks, plane * pair_slots, side)
    )
    held, flips = fresh[None], [0]
    mask = devices // 2
    while mask >= plane:
        held = jnp.concatenate([held, flip(held, mask)], axis=0)
        flips = flips + [f ^ (mask // plane) for f in flips]
        mask //= 2
    trained = pl.pallas_call(
        lambda device_ref, *refs: trained_kernel(device_ref, plane, flips, *refs),
        out_shape=jax.ShapeDtypeStruct((plane * pair_slots, blocks * side), BF16),
        in_specs=[pl.BlockSpec(memory_space=pltpu.SMEM)] + vmem(2),
        out_specs=vmem(1)[0],
        compiler_params=PARAMS,
    )(device_ref, rows, held)
    planes = [[z * plane + i for i in range(plane)] for z in range(depth)]
    trained = lax.all_to_all(
        trained.reshape(plane, pair_slots, blocks * side),
        "dp",
        split_axis=0,
        concat_axis=0,
        tiled=True,
        axis_index_groups=planes,
    )
    decoded = pl.pallas_call(
        combine_kernel,
        out_shape=jax.ShapeDtypeStruct((steps * step_rows, columns), BF16),
        in_specs=vmem(4),
        out_specs=vmem(1)[0],
        compiler_params=PARAMS,
    )(returned, trained, gates, gates_trained)
    return (decoded.reshape(steps, step_rows, columns), new_master)


def solution(mesh):
    return jax.shard_map(
        local,
        mesh=mesh,
        in_specs=(
            P(("groups", "dp"), None),
            P(("groups", "dp"), None),
            P("dp", None, None),
            P("dp", None, None),
            P("dp", None, None),
            P("dp", None),
            P("dp", None),
            P(),
            P(None, ("groups", "dp"), None, None),
            P(None, ("groups", "dp"), None),
            P(None, ("groups", "dp"), None),
        ),
        out_specs=(P(None, ("groups", "dp"), None), P(("groups", "dp"), None, None)),
        check_vma=False,
    )
```

```python
import jax
import jax.numpy as jnp
from jax import lax
from jax.experimental import pallas as pl
from jax.experimental.pallas import tpu as pltpu
from jax.sharding import PartitionSpec as P

learn_rate = 0.05
beta_first = 0.9
beta_second = 0.95
correct_first = 1.0 - 0.9**10
correct_second = 1.0 - 0.95**10
decay_rate = 0.1
adam_epsilon = 1e-08
quant_range = 448.0

F32 = jnp.float32
BF16 = jnp.bfloat16
PARAMS = pltpu.CompilerParams(vmem_limit_bytes=16 * 2**20)


def optimizer(gradient, master, moment_first, moment_second):
    first_moment = beta_first * moment_first + (1.0 - beta_first) * gradient
    second_moment = beta_second * moment_second + (1.0 - beta_second) * gradient * gradient
    update = (
        first_moment / correct_first / (jnp.sqrt(second_moment / correct_second) + adam_epsilon)
    )
    return master - learn_rate * (update + decay_rate * master)


def update_kernel(master, moment_first, moment_second, *rest):
    parts, new_master, fresh = rest[:-2], rest[-2], rest[-1]
    for block in range(master.shape[0]):
        gradient = parts[0][block].astype(F32)
        for part in parts[1:]:
            gradient = gradient + part[block].astype(F32)
        weights = optimizer(gradient, master[block], moment_first[block], moment_second[block])
        new_master[block] = weights
        largest = jnp.max(jnp.abs(weights), axis=(0, 1), keepdims=True)
        scale = (largest + 1e-06) / quant_range
        quantized = (weights / scale).astype(BF16)
        fresh[block] = (quantized.astype(F32) * scale).astype(BF16)


def in_hbm(*arrays):
    return [pltpu.with_memory_space_constraint(array, pltpu.HBM) for array in arrays]


def vmem(count):
    return [pl.BlockSpec(memory_space=pltpu.VMEM)] * count


def pack_kernel(
    steps,
    capacity,
    depth,
    placement,
    routing,
    gate_weight,
    hidden,
    packed,
    gates_trained,
    rows_trained,
):
    rows, topk = routing.shape
    entries = rows * topk
    step_entries = entries // steps
    experts = placement.shape[0]
    chips = experts // depth
    pair_slots = steps * capacity

    def iota(shape, axis):
        return lax.broadcasted_iota(jnp.int32, shape, axis)

    def ones(mask):
        return jnp.where(mask, 1.0, 0.0).astype(BF16)

    spread = ones(iota((topk, entries), 1) % topk == iota((topk, entries), 0))
    mine = iota((rows, entries), 1) // topk == iota((rows, entries), 0)

    def along(values):
        return jnp.where(mine, jnp.dot(values, spread, preferred_element_type=F32), 0.0)

    routed = jnp.sum(along(routing[...].astype(F32).astype(BF16)), axis=0, keepdims=True)
    routed = routed.astype(jnp.int32)
    named = ones(iota((experts, entries), 0) == routed)
    same = lax.dot_general(named, named, (((0,), (0,)), ((), ())), preferred_element_type=F32)
    lane, line = iota((entries, entries), 1), iota((entries, entries), 0)
    earlier = (lane // step_entries == line // step_entries) & (line // topk < lane // topk)
    place = jnp.sum(jnp.where(earlier, same, 0.0), axis=0, keepdims=True).astype(jnp.int32)
    pair = jnp.zeros_like(routed)
    for expert in range(experts):
        pair = jnp.where(routed == expert, placement[expert], pair)
    entry = lax.broadcasted_iota(jnp.int32, (1, entries), 1)
    step_slot = entry // step_entries * capacity + place
    chip = pair % chips * depth
    slot = (chip + pair // chips) * pair_slots + step_slot
    slots = experts * pair_slots
    slot_line = lax.broadcasted_iota(jnp.int32, (slots, entries), 0)
    onehot = jnp.where(slot_line == slot, 1.0, 0.0).astype(BF16)
    width = hidden.shape[1]
    packed[:, :width] = jnp.dot(
        onehot, hidden[...], preferred_element_type=F32
    ).astype(BF16)
    onehot_trained = ones((iota((pair_slots, entries), 0) == step_slot) & (routed == 0))
    rows_trained[...] = jnp.dot(
        onehot_trained, hidden[...], preferred_element_type=F32
    ).astype(BF16)
    weight = gate_weight[...]
    high = weight.astype(BF16)
    rest = (weight - high.astype(F32)).astype(BF16)
    both = jnp.concatenate([along(high), along(rest)], axis=0).astype(BF16)
    over_entries = (((1,), (1,)), ((), ()))
    gates_trained[...] = lax.dot_general(
        both, onehot_trained, over_entries, preferred_element_type=F32
    ).astype(BF16)
    counted = jnp.where(routed == 0, 0.0, both.astype(F32)).astype(BF16)
    unused = jnp.zeros((packed.shape[1] - width - 2 * rows, entries), BF16)
    packed[:, width:] = lax.dot_general(
        onehot,
        jnp.concatenate([counted, unused], axis=0),
        over_entries,
        preferred_element_type=F32,
    ).astype(BF16)


def gradient_kernel(
    device_ref, hidden_own, hidden_other, cotangent_own, cotangent_other, *rest
):
    outs, hidden_across, cotangent = rest[:8], rest[8], rest[9]
    device = device_ref[0]
    tokens = hidden_own.shape[0]
    hidden_across[:, :tokens] = hidden_own[...].T
    hidden_across[:, tokens:] = hidden_other[...].T
    cotangent[:tokens] = cotangent_own[...]
    cotangent[tokens:] = cotangent_other[...]
    highs, blocks, side, _ = outs[0].shape
    column_blocks = cotangent.shape[1] // side
    wide = 2 if blocks % 2 == 0 else 1
    core = device % 2
    bit_x = device // 2 % 2
    bit_y = device // 4 % 2
    for part in range(4):
        for half in range(2):
            first, second = part < 2, part % 2 == 0
            over_x, over_y = (first, second) if half == 0 else (second, first)
            x = 1 - bit_x if over_x else bit_x
            y = 1 - bit_y if over_y else bit_y
            out = outs[4 * half + part]
            for high in range(highs):
                dest = (((high + half * highs) * 2 + y) * 2 + x) * 2 + core
                for at in range(0, blocks, wide):
                    block = dest * blocks + at
                    row = pl.multiple_of(block // column_blocks * side, side)
                    column = pl.multiple_of(block % column_blocks * side, side)
                    product = jnp.dot(
                        hidden_across[pl.ds(row, side), :],
                        cotangent[:, pl.ds(column, wide * side)],
                        preferred_element_type=F32,
                    ).astype(out.dtype)
                    for piece in range(wide):
                        out[high, at + piece] = product[:, piece * side : (piece + 1) * side]


def first_sum_kernel(arrived_a, held_a, arrived_b, held_b, out_a, out_b):
    out_a[...] = (arrived_a[...].astype(F32) + held_a[...].astype(F32)).astype(BF16)
    out_b[...] = (arrived_b[...].astype(F32) + held_b[...].astype(F32)).astype(BF16)


def second_sum_kernel(floor_ref, *rest):
    parts, outs, total = rest[:6], rest[6:10], rest[10]
    highs = parts[0].shape[0]
    for half in range(2):
        one, two, three = parts[3 * half : 3 * half + 3]
        total[half * highs : (half + 1) * highs] = (
            one[...].astype(F32) + two[...].astype(F32) + three[...].astype(F32)
        )
    for flip, out in zip((3, 1, 2, 0), outs, strict=True):
        out[...] = total[floor_ref[0] ^ flip].astype(out.dtype)


def third_sum_kernel(arrived, held, out):
    out[...] = (arrived[...].astype(F32) + held[...].astype(F32)).astype(BF16)


def expert_partial(rows, weights, scales):
    blocks, side = scales.shape[0], weights.shape[0] // scales.shape[0]
    scaled = [
        (weights[at * side : (at + 1) * side].astype(F32) * scales[at]).astype(BF16)
        for at in range(blocks)
    ]
    scaled = jnp.concatenate(scaled, axis=0)
    return jnp.dot(rows, scaled, preferred_element_type=F32).astype(BF16)


def expert_kernel(
    core_ref, rows, rows_trained, weights, weights_other, scales, scales_other, out
):
    half, wide = weights.shape
    step = pl.program_id(0)
    total = 0.0
    for core, kept, scale in (
        (core_ref[0], weights, scales),
        (1 - core_ref[0], weights_other, scales_other),
    ):
        at = pl.ds(pl.multiple_of(core * half, half), half)
        total = total + expert_partial(rows[:, at], kept, scale).astype(F32)
    chips = out.shape[0]
    count = rows.shape[0] // chips
    for chip in range(chips):
        out[chip, :count, pl.ds(pl.multiple_of(step * wide, wide), wide)] = total[
            chip * count : (chip + 1) * count
        ].astype(out.dtype)

    @pl.when(step == 0)
    def _():
        columns = wide * pl.num_programs(0)
        for chip in range(chips):
            out[chip, :count, columns:] = rows[chip * count : (chip + 1) * count, 2 * half :]
            out[chip, count:, : 2 * half] = rows_trained[...]
            out[chip, count:, 2 * half :] = jnp.zeros(
                (out.shape[1] - count, out.shape[2] - 2 * half), out.dtype
            )


def trained_kernel(device_ref, plane, depth, column_blocks, *rest):
    given, weights = rest[:2], rest[2 : 2 + depth]
    out, rows = rest[2 + depth :]
    device = device_ref[0]
    blocks, side, _ = weights[0].shape
    inner = device % plane
    floor = device // plane
    chips, count, _ = given[0].shape
    for row_block in range(rows.shape[0]):
        at = slice(row_block * side, (row_block + 1) * side)
        rows[row_block] = jnp.concatenate(
            [part[chip, :, at] for part in given for chip in range(chips)], axis=0
        )
    for at in range(blocks):
        total = jnp.zeros((rows.shape[1], side), F32)
        for flip in range(depth):
            block = ((floor ^ flip) * plane + inner) * blocks + at
            row_block = block // column_blocks
            total = total + jnp.dot(rows[row_block], weights[flip][at], preferred_element_type=F32)
        for core in range(2):
            for chip in range(chips):
                top = (core * chips + chip) * count
                out[2 * chip + (device % 2 ^ core), :, at * side : (at + 1) * side] = total[
                    top : top + count
                ].astype(BF16)


def mix_kernel(depth, plane_slots, floor_ref, returned, *outs):
    count, columns = outs[0].shape

    def of_chips(at):
        return jnp.concatenate(
            [returned[chip, :plane_slots, at] for chip in range(returned.shape[0])], axis=0
        )

    gates = of_chips(slice(columns, None)).astype(F32)
    slot = lax.broadcasted_iota(jnp.int32, gates.shape, 0)
    plane = slot // (plane_slots // depth) % depth
    mine = [
        jnp.where(plane == (floor_ref[0] ^ flip), gates, 0.0).astype(BF16) for flip in range(depth)
    ]
    wide = 512
    for column in range(0, columns, wide):
        at = slice(column, column + wide)
        rows = of_chips(at)
        for flip, out in enumerate(outs):
            mixed = lax.dot_general(
                mine[flip], rows, (((0,), (0,)), ((), ())), preferred_element_type=F32
            )
            out[:, at] = (mixed[:count] + mixed[count : 2 * count]).astype(out.dtype)


def combine_kernel(depth, side, gates_trained, *rest):
    mixed, trained, out = rest[:depth], rest[depth], rest[depth + 1]
    peers, _, width = trained.shape
    columns = out.shape[1]
    blocks = width // side
    count = out.shape[0]
    wide = 4
    for column in range(0, columns // side, wide):
        fresh = []
        for place in range(column, column + wide):
            total = None
            for number in range(place, peers * blocks, columns // side):
                peer, block = divmod(number, blocks)
                piece = trained[peer, :, block * side : (block + 1) * side].astype(F32)
                total = piece if total is None else total + piece
            fresh.append(total.astype(BF16))
        at = slice(column * side, (column + wide) * side)
        both = jnp.dot(
            gates_trained[...], jnp.concatenate(fresh, axis=1), preferred_element_type=F32
        )
        total = both[:count] + both[count:]
        for part in mixed:
            total = total + part[:, at].astype(F32)
        out[:, at] = total.astype(out.dtype)


def local(
    learn_hidden,
    learn_cotangent,
    master,
    moment_first,
    moment_second,
    resident_weight,
    resident_scale,
    placement,
    decode_hidden,
    routing,
    gate_weight,
):
    devices = lax.axis_size("dp")
    device = lax.axis_index("dp")
    device_ref = device.astype(jnp.int32).reshape(1)
    blocks, side = master.shape[:2]
    hidden_width = learn_hidden.shape[1]
    columns = learn_cotangent.shape[1]
    row_blocks = hidden_width // side
    column_blocks = columns // side
    tokens = learn_hidden.shape[0]
    steps, step_rows, topk = routing.shape
    experts = placement.shape[0]
    capacity = min(step_rows, step_rows * topk // experts + 2)
    entries = steps * step_rows * topk
    pair_slots = steps * capacity
    slots = experts * pair_slots
    half = hidden_width // 2

    def flip(array, mask):
        return lax.ppermute(array, "dp", [(i, i ^ mask) for i in range(devices)])

    def bit(number):
        return device // 2**number % 2

    def after(array, *others):
        return lax.optimization_barrier((array, others))[0]

    def pick(array, index, axis):
        return lax.dynamic_index_in_dim(array, index, axis, keepdims=False)

    plane = 1
    while plane * blocks % column_blocks:
        plane *= 2
    depth = devices // plane
    chips = plane // 2
    floor_ref = (device // plane).astype(jnp.int32).reshape(1)
    row_count = steps * step_rows
    gate_lanes = -(-2 * row_count // 128) * 128
    smem = pl.BlockSpec(memory_space=pltpu.SMEM)

    packed, gates_trained, rows_trained = pl.pallas_call(
        lambda *refs: pack_kernel(steps, capacity, depth, *refs),
        out_shape=(
            pltpu.HBM((slots, hidden_width + gate_lanes), BF16),
            jax.ShapeDtypeStruct((2 * steps * step_rows, pair_slots), BF16),
            jax.ShapeDtypeStruct((pair_slots, hidden_width), BF16),
        ),
        in_specs=[smem] + vmem(3),
        out_specs=tuple(vmem(3)),
        compiler_params=PARAMS,
    )(
        placement,
        *in_hbm(
            routing.reshape(steps * step_rows, topk),
            gate_weight.reshape(steps * step_rows, topk),
            decode_hidden.reshape(entries, hidden_width),
        ),
    )
    hidden_other, cotangent_other = flip(learn_hidden, 1), flip(learn_cotangent, 1)
    same_core = [
        [z * plane + chip * 2 + core for chip in range(chips) for z in range(depth)]
        for core in range(2)
    ]
    received = lax.all_to_all(
        after(packed, hidden_other, cotangent_other).reshape(
            experts, pair_slots, hidden_width + gate_lanes
        ),
        "dp",
        split_axis=0,
        concat_axis=0,
        tiled=True,
        axis_index_groups=same_core,
    ).reshape(slots, hidden_width + gate_lanes)

    highs = devices // 16
    part = jax.ShapeDtypeStruct((highs, blocks, side, side), BF16)
    parts = pl.pallas_call(
        gradient_kernel,
        out_shape=(pltpu.HBM(part.shape, BF16),) * 8,
        in_specs=[smem] + vmem(4),
        out_specs=tuple(vmem(8)),
        scratch_shapes=[
            pltpu.VMEM((hidden_width, 2 * tokens), BF16),
            pltpu.VMEM((2 * tokens, columns), BF16),
        ],
        compiler_params=PARAMS,
    )(
        device_ref,
        *in_hbm(after(learn_hidden, packed), hidden_other, learn_cotangent, cotangent_other),
    )
    both_a, first_a, second_a, stay_a, both_b, first_b, second_b, stay_b = parts
    both_a, both_b = flip(both_a, 2), flip(both_b, 4)
    first_a, first_b = flip(first_a, 2), flip(first_b, 4)
    weights_other = flip(after(resident_weight, hidden_other, cotangent_other), 1)
    scales_other = flip(resident_scale, 1)
    second_a = after(second_a, weights_other)
    second_a, second_b = pl.pallas_call(
        first_sum_kernel,
        out_shape=(pltpu.HBM(part.shape, BF16),) * 2,
        in_specs=vmem(4),
        out_specs=tuple(vmem(2)),
        compiler_params=PARAMS,
    )(both_a, second_a, both_b, second_b)
    sums = second_a, second_b
    second_a, second_b = flip(second_a, 4), flip(second_b, 2)

    plane_slots = depth * pair_slots
    sent_shape = (chips, plane_slots + pair_slots, columns + gate_lanes)

    def expert_sum(rows):
        wide = 512
        weight_spec = pl.BlockSpec((half, wide), lambda i, core: (0, i))
        scale_spec = pl.BlockSpec((row_blocks // 2, 1, wide), lambda i, core: (0, 0, i))
        return pl.pallas_call(
            expert_kernel,
            out_shape=pltpu.HBM(sent_shape, BF16),
            grid_spec=pltpu.PrefetchScalarGridSpec(
                num_scalar_prefetch=1,
                grid=(columns // wide,),
                in_specs=[
                    pl.BlockSpec((slots, hidden_width + gate_lanes), lambda i, core: (0, 0)),
                    pl.BlockSpec((pair_slots, hidden_width), lambda i, core: (0, 0)),
                    weight_spec,
                    weight_spec,
                    scale_spec,
                    scale_spec,
                ],
                out_specs=pl.BlockSpec(sent_shape, lambda i, core: (0, 0, 0)),
            ),
            compiler_params=PARAMS,
        )(
            bit(0).astype(jnp.int32).reshape(1),
            rows,
            rows_trained,
            resident_weight,
            weights_other,
            *(
                jnp.repeat(scales, side, axis=1)[:, None, :]
                for scales in (resident_scale, scales_other)
            ),
        )

    block_shape = (blocks, side, side)
    if highs == 2:
        expert_out = expert_sum(after(received, sums, first_a, first_b))
        expert_out = after(expert_out, second_a, second_b)
        far, near, across, own = pl.pallas_call(
            second_sum_kernel,
            out_shape=(
                pltpu.HBM(block_shape, BF16),
                pltpu.HBM(block_shape, BF16),
                pltpu.HBM(block_shape, F32),
                pltpu.HBM(block_shape, F32),
            ),
            in_specs=[smem] + vmem(6),
            out_specs=tuple(vmem(4)),
            scratch_shapes=[pltpu.VMEM((4,) + block_shape, F32)],
            compiler_params=PARAMS,
        )(
            (device // 8).astype(jnp.int32).reshape(1),
            stay_a,
            first_a,
            second_a,
            stay_b,
            first_b,
            second_b,
        )
        far, near = flip(far, 8), flip(near, 8)
        across = pl.pallas_call(
            third_sum_kernel,
            out_shape=jax.ShapeDtypeStruct(block_shape, BF16),
            in_specs=vmem(2),
            out_specs=vmem(1)[0],
            compiler_params=PARAMS,
        )(far, across)
        gradient = [own, near, flip(across, 16)]
    else:
        expert_out = expert_sum(received)
        sums = [
            sum(piece.astype(F32) for piece in pieces)
            for pieces in ((stay_a, first_a, second_a), (stay_b, first_b, second_b))
        ]
        total = jnp.concatenate(sums, axis=0)
        number = 3
        while total.shape[0] > 1:
            split = total.reshape((-1, 2) + block_shape)
            sent = pick(split, 1 - bit(number), 1).astype(BF16)
            total = pick(split, bit(number), 1) + flip(sent, 2**number).astype(F32)
            number += 1
        gradient = [total[0]]
    new_master, fresh = pl.pallas_call(
        update_kernel,
        out_shape=(
            jax.ShapeDtypeStruct(block_shape, F32),
            jax.ShapeDtypeStruct(block_shape, BF16),
        ),
        in_specs=vmem(3 + len(gradient)),
        out_specs=tuple(vmem(2)),
        compiler_params=PARAMS,
    )(master, moment_first, moment_second, *gradient)

    same_core = [
        [z * plane + chip * 2 + core for chip in range(chips)]
        for z in range(depth)
        for core in range(2)
    ]
    returned = lax.all_to_all(
        expert_out, "dp", split_axis=0, concat_axis=0, tiled=True, axis_index_groups=same_core
    )
    rows_trained = returned[:, plane_slots:, :hidden_width]
    rows_other = flip(rows_trained, 1)
    mixed = pl.pallas_call(
        lambda *refs: mix_kernel(depth, plane_slots, *refs),
        out_shape=(jax.ShapeDtypeStruct((row_count, columns), F32),)
        + (jax.ShapeDtypeStruct((row_count, columns), BF16),) * (depth - 1),
        in_specs=[smem] + vmem(1),
        out_specs=tuple(vmem(depth)),
        compiler_params=PARAMS,
    )(floor_ref, after(returned, fresh))
    mixed = [mixed[0]] + [flip(mixed[z], z * plane) for z in range(1, depth)]

    held = {0: fresh}
    mask = depth // 2
    while mask:
        for key in list(held):
            held[key | mask] = flip(held[key], mask * plane)
        mask //= 2
    trained = pl.pallas_call(
        lambda device_ref, *refs: trained_kernel(device_ref, plane, depth, column_blocks, *refs),
        out_shape=pltpu.HBM((plane, pair_slots, blocks * side), BF16),
        in_specs=[smem] + vmem(2 + depth),
        out_specs=vmem(1)[0],
        scratch_shapes=[pltpu.VMEM((row_blocks, plane * pair_slots, side), BF16)],
        compiler_params=PARAMS,
    )(device_ref, after(rows_trained, mixed[0]), rows_other, *[held[z] for z in range(depth)])
    planes = [[z * plane + i for i in range(plane)] for z in range(depth)]
    trained = lax.all_to_all(
        trained, "dp", split_axis=0, concat_axis=0, tiled=True, axis_index_groups=planes
    )
    decoded = pl.pallas_call(
        lambda *refs: combine_kernel(depth, side, *refs),
        out_shape=jax.ShapeDtypeStruct((row_count, columns), BF16),
        in_specs=vmem(2 + depth),
        out_specs=vmem(1)[0],
        compiler_params=PARAMS,
    )(gates_trained, *mixed, trained)
    return (decoded.reshape(steps, step_rows, columns), new_master)


def solution(mesh):
    return jax.shard_map(
        local,
        mesh=mesh,
        in_specs=(
            P(("groups", "dp"), None),
            P(("groups", "dp"), None),
            P("dp", None, None),
            P("dp", None, None),
            P("dp", None, None),
            P("dp", None),
            P("dp", None),
            P(),
            P(None, ("groups", "dp"), None, None),
            P(None, ("groups", "dp"), None),
            P(None, ("groups", "dp"), None),
        ),
        out_specs=(P(None, ("groups", "dp"), None), P(("groups", "dp"), None, None)),
        check_vma=False,
    )
```

```python
import jax
import jax.numpy as jnp
from jax import lax
from jax.experimental import pallas as pl
from jax.experimental.pallas import tpu as pltpu
from jax.sharding import PartitionSpec as P

learn_rate = 0.05
beta_first = 0.9
beta_second = 0.95
correct_first = 1.0 - 0.9**10
correct_second = 1.0 - 0.95**10
decay_rate = 0.1
adam_epsilon = 1e-08
quant_range = 448.0

F32 = jnp.float32
BF16 = jnp.bfloat16
PARAMS = pltpu.CompilerParams(vmem_limit_bytes=16 * 2**20)


def optimizer(gradient, master, moment_first, moment_second):
    first_moment = beta_first * moment_first + (1.0 - beta_first) * gradient
    second_moment = beta_second * moment_second + (1.0 - beta_second) * gradient * gradient
    update = (
        first_moment / correct_first / (jnp.sqrt(second_moment / correct_second) + adam_epsilon)
    )
    return master - learn_rate * (update + decay_rate * master)


def update_kernel(master, moment_first, moment_second, *rest):
    parts, new_master, fresh = rest[:-2], rest[-2], rest[-1]
    for block in range(master.shape[0]):
        gradient = parts[0][block].astype(F32)
        for part in parts[1:]:
            gradient = gradient + part[block].astype(F32)
        weights = optimizer(gradient, master[block], moment_first[block], moment_second[block])
        new_master[block] = weights
        largest = jnp.max(jnp.abs(weights), axis=(0, 1), keepdims=True)
        scale = (largest + 1e-06) / quant_range
        quantized = (weights / scale).astype(BF16)
        fresh[block] = (quantized.astype(F32) * scale).astype(BF16)


def in_hbm(*arrays):
    return [pltpu.with_memory_space_constraint(array, pltpu.HBM) for array in arrays]


def vmem(count):
    return [pl.BlockSpec(memory_space=pltpu.VMEM)] * count


def pack_kernel(
    steps,
    capacity,
    depth,
    placement,
    routing,
    gate_weight,
    hidden,
    packed,
    gates_trained,
    rows_trained,
):
    rows, topk = routing.shape
    entries = rows * topk
    step_entries = entries // steps
    experts = placement.shape[0]
    chips = experts // depth
    pair_slots = steps * capacity

    def iota(shape, axis):
        return lax.broadcasted_iota(jnp.int32, shape, axis)

    def ones(mask):
        return jnp.where(mask, 1.0, 0.0).astype(BF16)

    spread = ones(iota((topk, entries), 1) % topk == iota((topk, entries), 0))
    mine = iota((rows, entries), 1) // topk == iota((rows, entries), 0)

    def along(values):
        return jnp.where(mine, jnp.dot(values, spread, preferred_element_type=F32), 0.0)

    routed = jnp.sum(along(routing[...].astype(F32).astype(BF16)), axis=0, keepdims=True)
    routed = routed.astype(jnp.int32)
    named = ones(iota((experts, entries), 0) == routed)
    same = lax.dot_general(named, named, (((0,), (0,)), ((), ())), preferred_element_type=F32)
    lane, line = iota((entries, entries), 1), iota((entries, entries), 0)
    earlier = (lane // step_entries == line // step_entries) & (line // topk < lane // topk)
    place = jnp.sum(jnp.where(earlier, same, 0.0), axis=0, keepdims=True).astype(jnp.int32)
    pair = jnp.zeros_like(routed)
    for expert in range(experts):
        pair = jnp.where(routed == expert, placement[expert], pair)
    entry = lax.broadcasted_iota(jnp.int32, (1, entries), 1)
    step_slot = entry // step_entries * capacity + place
    chip = pair % chips * depth
    slot = (chip + pair // chips) * pair_slots + step_slot
    slots = experts * pair_slots
    slot_line = lax.broadcasted_iota(jnp.int32, (slots, entries), 0)
    onehot = jnp.where(slot_line == slot, 1.0, 0.0).astype(BF16)
    width = hidden.shape[1]
    packed[:, :width] = jnp.dot(
        onehot, hidden[...], preferred_element_type=F32
    ).astype(BF16)
    onehot_trained = ones((iota((pair_slots, entries), 0) == step_slot) & (routed == 0))
    rows_trained[...] = jnp.dot(
        onehot_trained, hidden[...], preferred_element_type=F32
    ).astype(BF16)
    weight = gate_weight[...]
    high = weight.astype(BF16)
    rest = (weight - high.astype(F32)).astype(BF16)
    both = jnp.concatenate([along(high), along(rest)], axis=0).astype(BF16)
    over_entries = (((1,), (1,)), ((), ()))
    gates_trained[...] = lax.dot_general(
        both, onehot_trained, over_entries, preferred_element_type=F32
    ).astype(BF16)
    counted = jnp.where(routed == 0, 0.0, both.astype(F32)).astype(BF16)
    unused = jnp.zeros((packed.shape[1] - width - 2 * rows, entries), BF16)
    packed[:, width:] = lax.dot_general(
        onehot,
        jnp.concatenate([counted, unused], axis=0),
        over_entries,
        preferred_element_type=F32,
    ).astype(BF16)


def gradient_kernel(
    device_ref, hidden_own, hidden_other, cotangent_own, cotangent_other, *rest
):
    outs, hidden_across, cotangent = rest[:8], rest[8], rest[9]
    device = device_ref[0]
    tokens = hidden_own.shape[0]
    hidden_across[:, :tokens] = hidden_own[...].T
    hidden_across[:, tokens:] = hidden_other[...].T
    cotangent[:tokens] = cotangent_own[...]
    cotangent[tokens:] = cotangent_other[...]
    highs, blocks, side, _ = outs[0].shape
    column_blocks = cotangent.shape[1] // side
    wide = 2 if blocks % 2 == 0 else 1
    core = device % 2
    bit_x = device // 2 % 2
    bit_y = device // 4 % 2
    for part in range(4):
        for half in range(2):
            first, second = part < 2, part % 2 == 0
            over_x, over_y = (first, second) if half == 0 else (second, first)
            x = 1 - bit_x if over_x else bit_x
            y = 1 - bit_y if over_y else bit_y
            out = outs[4 * half + part]
            for high in range(highs):
                dest = (((high + half * highs) * 2 + y) * 2 + x) * 2 + core
                for at in range(0, blocks, wide):
                    block = dest * blocks + at
                    row = pl.multiple_of(block // column_blocks * side, side)
                    column = pl.multiple_of(block % column_blocks * side, side)
                    product = jnp.dot(
                        hidden_across[pl.ds(row, side), :],
                        cotangent[:, pl.ds(column, wide * side)],
                        preferred_element_type=F32,
                    ).astype(out.dtype)
                    for piece in range(wide):
                        out[high, at + piece] = product[:, piece * side : (piece + 1) * side]


def first_sum_kernel(arrived_a, held_a, arrived_b, held_b, out_a, out_b):
    out_a[...] = (arrived_a[...].astype(F32) + held_a[...].astype(F32)).astype(BF16)
    out_b[...] = (arrived_b[...].astype(F32) + held_b[...].astype(F32)).astype(BF16)


def second_sum_kernel(floor_ref, *rest):
    parts, outs, total = rest[:6], rest[6:10], rest[10]
    highs = parts[0].shape[0]
    for half in range(2):
        one, two, three = parts[3 * half : 3 * half + 3]
        total[half * highs : (half + 1) * highs] = (
            one[...].astype(F32) + two[...].astype(F32) + three[...].astype(F32)
        )
    for flip, out in zip((3, 1, 2, 0), outs, strict=True):
        out[...] = total[floor_ref[0] ^ flip].astype(out.dtype)


def third_sum_kernel(arrived, held, out):
    out[...] = (arrived[...].astype(F32) + held[...].astype(F32)).astype(BF16)


def expert_partial(rows, weights, scales):
    blocks, side = scales.shape[0], weights.shape[0] // scales.shape[0]
    scaled = [
        (weights[at * side : (at + 1) * side].astype(F32) * scales[at]).astype(BF16)
        for at in range(blocks)
    ]
    scaled = jnp.concatenate(scaled, axis=0)
    return jnp.dot(rows, scaled, preferred_element_type=F32).astype(BF16)


def expert_kernel(
    core_ref, rows, rows_trained, weights, weights_other, scales, scales_other, out
):
    half, wide = weights.shape
    step = pl.program_id(0)
    total = 0.0
    for core, kept, scale in (
        (core_ref[0], weights, scales),
        (1 - core_ref[0], weights_other, scales_other),
    ):
        at = pl.ds(pl.multiple_of(core * half, half), half)
        total = total + expert_partial(rows[:, at], kept, scale).astype(F32)
    chips = out.shape[0]
    count = rows.shape[0] // chips
    for chip in range(chips):
        out[chip, :count, pl.ds(pl.multiple_of(step * wide, wide), wide)] = total[
            chip * count : (chip + 1) * count
        ].astype(out.dtype)

    @pl.when(step == 0)
    def _():
        columns = wide * pl.num_programs(0)
        for chip in range(chips):
            out[chip, :count, columns:] = rows[chip * count : (chip + 1) * count, 2 * half :]
            out[chip, count:, : 2 * half] = rows_trained[...]
            out[chip, count:, 2 * half :] = jnp.zeros(
                (out.shape[1] - count, out.shape[2] - 2 * half), out.dtype
            )


def trained_kernel(device_ref, plane, depth, column_blocks, *rest):
    given, weights = rest[:2], rest[2 : 2 + depth]
    out, rows = rest[2 + depth :]
    device = device_ref[0]
    blocks, side, _ = weights[0].shape
    inner = device % plane
    floor = device // plane
    chips, count, _ = given[0].shape
    for row_block in range(rows.shape[0]):
        at = slice(row_block * side, (row_block + 1) * side)
        rows[row_block] = jnp.concatenate(
            [part[chip, :, at] for part in given for chip in range(chips)], axis=0
        )
    for at in range(blocks):
        total = jnp.zeros((rows.shape[1], side), F32)
        for flip in range(depth):
            block = ((floor ^ flip) * plane + inner) * blocks + at
            row_block = block // column_blocks
            total = total + jnp.dot(rows[row_block], weights[flip][at], preferred_element_type=F32)
        for core in range(2):
            for chip in range(chips):
                top = (core * chips + chip) * count
                out[2 * chip + (device % 2 ^ core), :, at * side : (at + 1) * side] = total[
                    top : top + count
                ].astype(BF16)


def mix_kernel(depth, plane_slots, floor_ref, returned, own, across, sent):
    count, columns = own.shape
    outs = own, sent.at[0], across, sent.at[1]

    def of_chips(at):
        return jnp.concatenate(
            [returned[chip, :plane_slots, at] for chip in range(returned.shape[0])], axis=0
        )

    gates = of_chips(slice(columns, None)).astype(F32)
    slot = lax.broadcasted_iota(jnp.int32, gates.shape, 0)
    plane = slot // (plane_slots // depth) % depth
    mine = [
        jnp.where(plane == (floor_ref[0] ^ flip), gates, 0.0).astype(BF16) for flip in range(depth)
    ]
    wide = 512
    for column in range(0, columns, wide):
        at = slice(column, column + wide)
        rows = of_chips(at)
        for flip, out in enumerate(outs):
            mixed = lax.dot_general(
                mine[flip], rows, (((0,), (0,)), ((), ())), preferred_element_type=F32
            )
            out[:, at] = (mixed[:count] + mixed[count : 2 * count]).astype(out.dtype)


def mix_sum_kernel(arrived, across, own, out_across, out_own):
    out_across[...] = (arrived[1].astype(F32) + across[...]).astype(BF16)
    out_own[...] = arrived[0].astype(F32) + own[...]


def combine_kernel(side, gates_trained, near, across, trained, out):
    peers, _, width = trained.shape
    columns = out.shape[1]
    blocks = width // side
    count = out.shape[0]
    wide = 4
    for column in range(0, columns // side, wide):
        fresh = []
        for place in range(column, column + wide):
            total = None
            for number in range(place, peers * blocks, columns // side):
                peer, block = divmod(number, blocks)
                piece = trained[peer, :, block * side : (block + 1) * side].astype(F32)
                total = piece if total is None else total + piece
            fresh.append(total.astype(BF16))
        at = slice(column * side, (column + wide) * side)
        both = jnp.dot(
            gates_trained[...], jnp.concatenate(fresh, axis=1), preferred_element_type=F32
        )
        total = both[:count] + both[count:]
        total = total + near[:, at] + across[:, at].astype(F32)
        out[:, at] = total.astype(out.dtype)


def local(
    learn_hidden,
    learn_cotangent,
    master,
    moment_first,
    moment_second,
    resident_weight,
    resident_scale,
    placement,
    decode_hidden,
    routing,
    gate_weight,
):
    devices = lax.axis_size("dp")
    device = lax.axis_index("dp")
    device_ref = device.astype(jnp.int32).reshape(1)
    blocks, side = master.shape[:2]
    hidden_width = learn_hidden.shape[1]
    columns = learn_cotangent.shape[1]
    row_blocks = hidden_width // side
    column_blocks = columns // side
    tokens = learn_hidden.shape[0]
    steps, step_rows, topk = routing.shape
    experts = placement.shape[0]
    capacity = min(step_rows, step_rows * topk // experts + 2)
    entries = steps * step_rows * topk
    pair_slots = steps * capacity
    slots = experts * pair_slots
    half = hidden_width // 2

    def flip(array, mask):
        return lax.ppermute(array, "dp", [(i, i ^ mask) for i in range(devices)])

    def bit(number):
        return device // 2**number % 2

    def after(array, *others):
        return lax.optimization_barrier((array, others))[0]

    def pick(array, index, axis):
        return lax.dynamic_index_in_dim(array, index, axis, keepdims=False)

    plane = 1
    while plane * blocks % column_blocks:
        plane *= 2
    depth = devices // plane
    chips = plane // 2
    floor_ref = (device // plane).astype(jnp.int32).reshape(1)
    row_count = steps * step_rows
    gate_lanes = -(-2 * row_count // 128) * 128
    smem = pl.BlockSpec(memory_space=pltpu.SMEM)

    packed, gates_trained, rows_trained = pl.pallas_call(
        lambda *refs: pack_kernel(steps, capacity, depth, *refs),
        out_shape=(
            pltpu.HBM((slots, hidden_width + gate_lanes), BF16),
            jax.ShapeDtypeStruct((2 * steps * step_rows, pair_slots), BF16),
            jax.ShapeDtypeStruct((pair_slots, hidden_width), BF16),
        ),
        in_specs=[smem] + vmem(3),
        out_specs=tuple(vmem(3)),
        compiler_params=PARAMS,
    )(
        placement,
        *in_hbm(
            routing.reshape(steps * step_rows, topk),
            gate_weight.reshape(steps * step_rows, topk),
            decode_hidden.reshape(entries, hidden_width),
        ),
    )
    hidden_other, cotangent_other = flip(learn_hidden, 1), flip(learn_cotangent, 1)
    same_core = [
        [z * plane + chip * 2 + core for chip in range(chips) for z in range(depth)]
        for core in range(2)
    ]
    received = lax.all_to_all(
        after(packed, hidden_other, cotangent_other).reshape(
            experts, pair_slots, hidden_width + gate_lanes
        ),
        "dp",
        split_axis=0,
        concat_axis=0,
        tiled=True,
        axis_index_groups=same_core,
    ).reshape(slots, hidden_width + gate_lanes)

    highs = devices // 16
    part = jax.ShapeDtypeStruct((highs, blocks, side, side), BF16)
    parts = pl.pallas_call(
        gradient_kernel,
        out_shape=(pltpu.HBM(part.shape, BF16),) * 8,
        in_specs=[smem] + vmem(4),
        out_specs=tuple(vmem(8)),
        scratch_shapes=[
            pltpu.VMEM((hidden_width, 2 * tokens), BF16),
            pltpu.VMEM((2 * tokens, columns), BF16),
        ],
        compiler_params=PARAMS,
    )(
        device_ref,
        *in_hbm(after(learn_hidden, packed), hidden_other, learn_cotangent, cotangent_other),
    )
    both_a, first_a, second_a, stay_a, both_b, first_b, second_b, stay_b = parts
    both_a, both_b = flip(both_a, 2), flip(both_b, 4)
    first_a, first_b = flip(first_a, 2), flip(first_b, 4)
    weights_other = flip(after(resident_weight, packed, hidden_other, cotangent_other), 1)
    scales_other = flip(resident_scale, 1)
    second_a = after(second_a, weights_other)
    second_a, second_b = pl.pallas_call(
        first_sum_kernel,
        out_shape=(pltpu.HBM(part.shape, BF16),) * 2,
        in_specs=vmem(4),
        out_specs=tuple(vmem(2)),
        compiler_params=PARAMS,
    )(both_a, *in_hbm(second_a), both_b, *in_hbm(second_b))
    sums = second_a, second_b
    second_a, second_b = flip(second_a, 4), flip(second_b, 2)

    plane_slots = depth * pair_slots
    sent_shape = (chips, plane_slots + pair_slots, columns + gate_lanes)

    def expert_sum(rows):
        wide = 512
        weight_spec = pl.BlockSpec((half, wide), lambda i, core: (0, i))
        scale_spec = pl.BlockSpec((row_blocks // 2, 1, wide), lambda i, core: (0, 0, i))
        return pl.pallas_call(
            expert_kernel,
            out_shape=pltpu.HBM(sent_shape, BF16),
            grid_spec=pltpu.PrefetchScalarGridSpec(
                num_scalar_prefetch=1,
                grid=(columns // wide,),
                in_specs=[
                    pl.BlockSpec((slots, hidden_width + gate_lanes), lambda i, core: (0, 0)),
                    pl.BlockSpec((pair_slots, hidden_width), lambda i, core: (0, 0)),
                    weight_spec,
                    weight_spec,
                    scale_spec,
                    scale_spec,
                ],
                out_specs=pl.BlockSpec(sent_shape, lambda i, core: (0, 0, 0)),
            ),
            compiler_params=PARAMS,
        )(
            bit(0).astype(jnp.int32).reshape(1),
            rows,
            rows_trained,
            resident_weight,
            weights_other,
            *(
                jnp.repeat(scales, side, axis=1)[:, None, :]
                for scales in (resident_scale, scales_other)
            ),
        )

    block_shape = (blocks, side, side)
    if highs == 2:
        expert_out = expert_sum(after(received, sums, first_a, first_b))
        far, near, across, own = pl.pallas_call(
            second_sum_kernel,
            out_shape=(
                pltpu.HBM(block_shape, BF16),
                pltpu.HBM(block_shape, BF16),
                pltpu.HBM(block_shape, F32),
                pltpu.HBM(block_shape, F32),
            ),
            in_specs=[smem] + vmem(6),
            out_specs=tuple(vmem(4)),
            scratch_shapes=[pltpu.VMEM((4,) + block_shape, F32)],
            compiler_params=PARAMS,
        )(
            (device // 8).astype(jnp.int32).reshape(1),
            *in_hbm(stay_a),
            first_a,
            second_a,
            *in_hbm(stay_b),
            first_b,
            second_b,
        )
        expert_out = after(expert_out, own)
        far, near = flip(far, 8), flip(near, 8)
        across = pl.pallas_call(
            third_sum_kernel,
            out_shape=jax.ShapeDtypeStruct(block_shape, BF16),
            in_specs=vmem(2),
            out_specs=vmem(1)[0],
            compiler_params=PARAMS,
        )(far, *in_hbm(across))
        gradient = [own, near, flip(across, 16)]
    else:
        expert_out = expert_sum(received)
        sums = [
            sum(piece.astype(F32) for piece in pieces)
            for pieces in ((stay_a, first_a, second_a), (stay_b, first_b, second_b))
        ]
        total = jnp.concatenate(sums, axis=0)
        number = 3
        while total.shape[0] > 1:
            split = total.reshape((-1, 2) + block_shape)
            sent = pick(split, 1 - bit(number), 1).astype(BF16)
            total = pick(split, bit(number), 1) + flip(sent, 2**number).astype(F32)
            number += 1
        gradient = [total[0]]
    new_master, fresh = pl.pallas_call(
        update_kernel,
        out_shape=(
            jax.ShapeDtypeStruct(block_shape, F32),
            jax.ShapeDtypeStruct(block_shape, BF16),
        ),
        in_specs=vmem(3 + len(gradient)),
        out_specs=tuple(vmem(2)),
        compiler_params=PARAMS,
    )(master, moment_first, moment_second, *gradient)

    same_core = [
        [z * plane + chip * 2 + core for chip in range(chips)]
        for z in range(depth)
        for core in range(2)
    ]
    returned = lax.all_to_all(
        expert_out, "dp", split_axis=0, concat_axis=0, tiled=True, axis_index_groups=same_core
    )
    rows_trained = returned[:, plane_slots:, :hidden_width]
    rows_other = flip(rows_trained, 1)
    row_shape = (row_count, columns)
    mixed, across_rows, sent_rows = pl.pallas_call(
        lambda *refs: mix_kernel(depth, plane_slots, *refs),
        out_shape=(
            jax.ShapeDtypeStruct(row_shape, F32),
            jax.ShapeDtypeStruct(row_shape, F32),
            jax.ShapeDtypeStruct((2,) + row_shape, BF16),
        ),
        in_specs=[smem] + vmem(1),
        out_specs=tuple(vmem(3)),
        compiler_params=PARAMS,
    )(floor_ref, after(returned, fresh))
    sent_rows = flip(sent_rows, plane)
    across_rows, mixed_near = pl.pallas_call(
        mix_sum_kernel,
        out_shape=(
            jax.ShapeDtypeStruct(row_shape, BF16),
            jax.ShapeDtypeStruct(row_shape, F32),
        ),
        in_specs=vmem(3),
        out_specs=tuple(vmem(2)),
        compiler_params=PARAMS,
    )(sent_rows, across_rows, mixed)
    across_rows = flip(across_rows, 2 * plane)

    held = {0: fresh}
    mask = depth // 2
    while mask:
        for key in list(held):
            held[key | mask] = flip(held[key], mask * plane)
        mask //= 2
    trained = pl.pallas_call(
        lambda device_ref, *refs: trained_kernel(device_ref, plane, depth, column_blocks, *refs),
        out_shape=pltpu.HBM((plane, pair_slots, blocks * side), BF16),
        in_specs=[smem] + vmem(2 + depth),
        out_specs=vmem(1)[0],
        scratch_shapes=[pltpu.VMEM((row_blocks, plane * pair_slots, side), BF16)],
        compiler_params=PARAMS,
    )(device_ref, after(rows_trained, mixed), rows_other, *[held[z] for z in range(depth)])
    planes = [[z * plane + i for i in range(plane)] for z in range(depth)]
    trained = lax.all_to_all(
        trained, "dp", split_axis=0, concat_axis=0, tiled=True, axis_index_groups=planes
    )
    decoded = pl.pallas_call(
        lambda *refs: combine_kernel(side, *refs),
        out_shape=jax.ShapeDtypeStruct((row_count, columns), BF16),
        in_specs=vmem(4),
        out_specs=vmem(1)[0],
        compiler_params=PARAMS,
    )(gates_trained, mixed_near, across_rows, trained)
    return (decoded.reshape(steps, step_rows, columns), new_master)


def solution(mesh):
    return jax.shard_map(
        local,
        mesh=mesh,
        in_specs=(
            P(("groups", "dp"), None),
            P(("groups", "dp"), None),
            P("dp", None, None),
            P("dp", None, None),
            P("dp", None, None),
            P("dp", None),
            P("dp", None),
            P(),
            P(None, ("groups", "dp"), None, None),
            P(None, ("groups", "dp"), None),
            P(None, ("groups", "dp"), None),
        ),
        out_specs=(P(None, ("groups", "dp"), None), P(("groups", "dp"), None, None)),
        check_vma=False,
    )
```

```python
import jax
import jax.numpy as jnp
from jax import lax
from jax.experimental import pallas as pl
from jax.experimental.pallas import tpu as pltpu
from jax.sharding import PartitionSpec as P

learn_rate = 0.05
beta_first = 0.9
beta_second = 0.95
correct_first = 1.0 - 0.9**10
correct_second = 1.0 - 0.95**10
decay_rate = 0.1
adam_epsilon = 1e-08
quant_range = 448.0

F32 = jnp.float32
BF16 = jnp.bfloat16
PARAMS = pltpu.CompilerParams(vmem_limit_bytes=16 * 2**20)


def optimizer(gradient, master, moment_first, moment_second):
    first_moment = beta_first * moment_first + (1.0 - beta_first) * gradient
    second_moment = beta_second * moment_second + (1.0 - beta_second) * gradient * gradient
    update = (
        first_moment / correct_first / (jnp.sqrt(second_moment / correct_second) + adam_epsilon)
    )
    return master - learn_rate * (update + decay_rate * master)


def update_kernel(master, moment_first, moment_second, *rest):
    parts, new_master, fresh = rest[:-2], rest[-2], rest[-1]
    for block in range(master.shape[0]):
        gradient = parts[0][block].astype(F32)
        for part in parts[1:]:
            gradient = gradient + part[block].astype(F32)
        weights = optimizer(gradient, master[block], moment_first[block], moment_second[block])
        new_master[block] = weights
        largest = jnp.max(jnp.abs(weights), axis=(0, 1), keepdims=True)
        scale = (largest + 1e-06) / quant_range
        quantized = (weights / scale).astype(BF16)
        fresh[block] = (quantized.astype(F32) * scale).astype(BF16)


def in_hbm(*arrays):
    return [pltpu.with_memory_space_constraint(array, pltpu.HBM) for array in arrays]


def vmem(count):
    return [pl.BlockSpec(memory_space=pltpu.VMEM)] * count


def pack_kernel(
    steps,
    capacity,
    depth,
    placement,
    routing,
    gate_weight,
    hidden,
    packed,
    gates_trained,
    rows_trained,
):
    rows, topk = routing.shape
    entries = rows * topk
    step_entries = entries // steps
    experts = placement.shape[0]
    chips = experts // depth
    pair_slots = steps * capacity

    def iota(shape, axis):
        return lax.broadcasted_iota(jnp.int32, shape, axis)

    def ones(mask):
        return jnp.where(mask, 1.0, 0.0).astype(BF16)

    spread = ones(iota((topk, entries), 1) % topk == iota((topk, entries), 0))
    mine = iota((rows, entries), 1) // topk == iota((rows, entries), 0)

    def along(values):
        return jnp.where(mine, jnp.dot(values, spread, preferred_element_type=F32), 0.0)

    routed = jnp.sum(along(routing[...].astype(F32).astype(BF16)), axis=0, keepdims=True)
    routed = routed.astype(jnp.int32)
    named = ones(iota((experts, entries), 0) == routed)
    same = lax.dot_general(named, named, (((0,), (0,)), ((), ())), preferred_element_type=F32)
    lane, line = iota((entries, entries), 1), iota((entries, entries), 0)
    earlier = (lane // step_entries == line // step_entries) & (line // topk < lane // topk)
    place = jnp.sum(jnp.where(earlier, same, 0.0), axis=0, keepdims=True).astype(jnp.int32)
    pair = jnp.zeros_like(routed)
    for expert in range(experts):
        pair = jnp.where(routed == expert, placement[expert], pair)
    entry = lax.broadcasted_iota(jnp.int32, (1, entries), 1)
    step_slot = entry // step_entries * capacity + place
    chip = pair % chips * depth
    slot = (chip + pair // chips) * pair_slots + step_slot
    slots = experts * pair_slots
    slot_line = lax.broadcasted_iota(jnp.int32, (slots, entries), 0)
    onehot = jnp.where(slot_line == slot, 1.0, 0.0).astype(BF16)
    width = hidden.shape[1]
    packed[:, :width] = jnp.dot(
        onehot, hidden[...], preferred_element_type=F32
    ).astype(BF16)
    onehot_trained = ones((iota((pair_slots, entries), 0) == step_slot) & (routed == 0))
    rows_trained[...] = jnp.dot(
        onehot_trained, hidden[...], preferred_element_type=F32
    ).astype(BF16)
    weight = gate_weight[...]
    high = weight.astype(BF16)
    rest = (weight - high.astype(F32)).astype(BF16)
    both = jnp.concatenate([along(high), along(rest)], axis=0).astype(BF16)
    over_entries = (((1,), (1,)), ((), ()))
    gates_trained[...] = lax.dot_general(
        both, onehot_trained, over_entries, preferred_element_type=F32
    ).astype(BF16)
    counted = jnp.where(routed == 0, 0.0, both.astype(F32)).astype(BF16)
    unused = jnp.zeros((packed.shape[1] - width - 2 * rows, entries), BF16)
    packed[:, width:] = lax.dot_general(
        onehot,
        jnp.concatenate([counted, unused], axis=0),
        over_entries,
        preferred_element_type=F32,
    ).astype(BF16)


def gradient_kernel(
    device_ref, hidden_own, hidden_other, cotangent_own, cotangent_other, *rest
):
    outs, hidden_across, cotangent = rest[:8], rest[8], rest[9]
    device = device_ref[0]
    tokens = hidden_own.shape[0]
    hidden_across[:, :tokens] = hidden_own[...].T
    hidden_across[:, tokens:] = hidden_other[...].T
    cotangent[:tokens] = cotangent_own[...]
    cotangent[tokens:] = cotangent_other[...]
    highs, blocks, side, _ = outs[0].shape
    column_blocks = cotangent.shape[1] // side
    wide = 2 if blocks % 2 == 0 else 1
    core = device % 2
    bit_x = device // 2 % 2
    bit_y = device // 4 % 2
    for part in range(4):
        for half in range(2):
            first, second = part < 2, part % 2 == 0
            over_x, over_y = (first, second) if half == 0 else (second, first)
            x = 1 - bit_x if over_x else bit_x
            y = 1 - bit_y if over_y else bit_y
            out = outs[4 * half + part]
            for high in range(highs):
                dest = (((high + half * highs) * 2 + y) * 2 + x) * 2 + core
                for at in range(0, blocks, wide):
                    block = dest * blocks + at
                    row = pl.multiple_of(block // column_blocks * side, side)
                    column = pl.multiple_of(block % column_blocks * side, side)
                    product = jnp.dot(
                        hidden_across[pl.ds(row, side), :],
                        cotangent[:, pl.ds(column, wide * side)],
                        preferred_element_type=F32,
                    ).astype(out.dtype)
                    for piece in range(wide):
                        out[high, at + piece] = product[:, piece * side : (piece + 1) * side]


def first_sum_kernel(arrived_a, held_a, arrived_b, held_b, out_a, out_b):
    out_a[...] = (arrived_a[...].astype(F32) + held_a[...].astype(F32)).astype(BF16)
    out_b[...] = (arrived_b[...].astype(F32) + held_b[...].astype(F32)).astype(BF16)


def far_sum_kernel(far_ref, *rest):
    parts, out = rest[:6], rest[6]
    for half in range(2):

        @pl.when(far_ref[0] // 2 == half)
        def _(pieces=parts[3 * half : 3 * half + 3]):
            one, two, three = (piece[0].astype(F32) for piece in pieces)
            out[...] = (one + two + three).astype(out.dtype)


def second_sum_kernel(floor_ref, *rest):
    parts, outs, total = rest[:6], rest[6:9], rest[9]
    highs = parts[0].shape[0]
    for half in range(2):
        one, two, three = parts[3 * half : 3 * half + 3]
        total[half * highs : (half + 1) * highs] = (
            one[...].astype(F32) + two[...].astype(F32) + three[...].astype(F32)
        )
    for flip, out in zip((1, 2, 0), outs, strict=True):
        out[...] = total[floor_ref[0] ^ flip].astype(out.dtype)


def third_sum_kernel(arrived, held, out):
    out[...] = (arrived[...].astype(F32) + held[...].astype(F32)).astype(BF16)


def expert_partial(rows, weights, scales):
    blocks, side = scales.shape[0], weights.shape[0] // scales.shape[0]
    scaled = [
        (weights[at * side : (at + 1) * side].astype(F32) * scales[at]).astype(BF16)
        for at in range(blocks)
    ]
    scaled = jnp.concatenate(scaled, axis=0)
    return jnp.dot(rows, scaled, preferred_element_type=F32).astype(BF16)


def expert_kernel(
    core_ref, rows, rows_trained, weights, weights_other, scales, scales_other, out
):
    half, wide = weights.shape
    step = pl.program_id(0)
    total = 0.0
    for core, kept, scale in (
        (core_ref[0], weights, scales),
        (1 - core_ref[0], weights_other, scales_other),
    ):
        at = pl.ds(pl.multiple_of(core * half, half), half)
        total = total + expert_partial(rows[:, at], kept, scale).astype(F32)
    chips = out.shape[0]
    count = rows.shape[0] // chips
    for chip in range(chips):
        out[chip, :count, pl.ds(pl.multiple_of(step * wide, wide), wide)] = total[
            chip * count : (chip + 1) * count
        ].astype(out.dtype)

    @pl.when(step == 0)
    def _():
        columns = wide * pl.num_programs(0)
        for chip in range(chips):
            out[chip, :count, columns:] = rows[chip * count : (chip + 1) * count, 2 * half :]
            out[chip, count:, : 2 * half] = rows_trained[...]
            out[chip, count:, 2 * half :] = jnp.zeros(
                (out.shape[1] - count, out.shape[2] - 2 * half), out.dtype
            )


def trained_kernel(device_ref, plane, depth, column_blocks, rows, *rest):
    weights, outs = rest[: 2 * depth], rest[2 * depth :]
    device = device_ref[0]
    blocks, side, _ = weights[0].shape
    floor = device // plane
    chip = device % plane // 2
    chips, count, _ = rows.shape
    for core in range(2):
        number = device % 2 ^ core
        for at in range(blocks):
            total = jnp.zeros((chips * count, side), F32)
            for flip in range(depth):
                block = (floor ^ flip) * plane * blocks + (chip * 2 + number) * blocks + at
                start = pl.multiple_of(block // column_blocks * side, side)
                part = jnp.concatenate(
                    [rows[chip ^ turn, :, pl.ds(start, side)] for turn in range(chips)], axis=0
                )
                total = total + jnp.dot(
                    part, weights[core * depth + flip][at], preferred_element_type=F32
                )
            column = pl.ds(pl.multiple_of((number * blocks + at) * side, side), side)
            for turn in range(chips):
                outs[turn][:, column] = total[turn * count : (turn + 1) * count].astype(BF16)


def mix_kernel(depth, plane_slots, floor_ref, returned, own, across, sent):
    count, columns = own.shape
    outs = own, sent.at[0], across, sent.at[1]

    def of_chips(at):
        return jnp.concatenate(
            [returned[chip, :plane_slots, at] for chip in range(returned.shape[0])], axis=0
        )

    gates = of_chips(slice(columns, None)).astype(F32)
    slot = lax.broadcasted_iota(jnp.int32, gates.shape, 0)
    plane = slot // (plane_slots // depth) % depth
    mine = [
        jnp.where(plane == (floor_ref[0] ^ flip), gates, 0.0).astype(BF16) for flip in range(depth)
    ]
    wide = 512
    for column in range(0, columns, wide):
        at = slice(column, column + wide)
        rows = of_chips(at)
        for flip, out in enumerate(outs):
            mixed = lax.dot_general(
                mine[flip], rows, (((0,), (0,)), ((), ())), preferred_element_type=F32
            )
            out[:, at] = (mixed[:count] + mixed[count : 2 * count]).astype(out.dtype)


def mix_sum_kernel(arrived, across, own, out_across, out_own):
    out_across[...] = (arrived[1].astype(F32) + across[...]).astype(BF16)
    out_own[...] = arrived[0].astype(F32) + own[...]


def combine_kernel(chip_ref, chips, side, gates_trained, near, across, *rest):
    trained, out, fresh = rest[:chips], rest[chips], rest[chips + 1]
    columns = out.shape[1]
    blocks = trained[0].shape[1] // side
    count = out.shape[0]
    fresh[...] = jnp.zeros_like(fresh)
    for turn in range(chips):
        for at in range(blocks):
            number = ((chip_ref[0] ^ turn) * blocks + at) % (columns // side)
            column = pl.ds(pl.multiple_of(number * side, side), side)
            fresh[:, column] += trained[turn][:, at * side : (at + 1) * side].astype(F32)
    wide = 512
    for column in range(0, columns, wide):
        at = slice(column, column + wide)
        both = jnp.dot(gates_trained[...], fresh[:, at].astype(BF16), preferred_element_type=F32)
        total = both[:count] + both[count:] + near[:, at] + across[:, at].astype(F32)
        out[:, at] = total.astype(out.dtype)


def local(
    learn_hidden,
    learn_cotangent,
    master,
    moment_first,
    moment_second,
    resident_weight,
    resident_scale,
    placement,
    decode_hidden,
    routing,
    gate_weight,
):
    devices = lax.axis_size("dp")
    device = lax.axis_index("dp")
    device_ref = device.astype(jnp.int32).reshape(1)
    blocks, side = master.shape[:2]
    hidden_width = learn_hidden.shape[1]
    columns = learn_cotangent.shape[1]
    row_blocks = hidden_width // side
    column_blocks = columns // side
    tokens = learn_hidden.shape[0]
    steps, step_rows, topk = routing.shape
    experts = placement.shape[0]
    capacity = min(step_rows, step_rows * topk // experts + 2)
    entries = steps * step_rows * topk
    pair_slots = steps * capacity
    slots = experts * pair_slots
    half = hidden_width // 2

    def flip(array, mask):
        return lax.ppermute(array, "dp", [(i, i ^ mask) for i in range(devices)])

    def bit(number):
        return device // 2**number % 2

    def after(array, *others):
        return lax.optimization_barrier((array, others))[0]

    def pick(array, index, axis):
        return lax.dynamic_index_in_dim(array, index, axis, keepdims=False)

    plane = 1
    while plane * blocks % column_blocks:
        plane *= 2
    depth = devices // plane
    chips = plane // 2
    floor_ref = (device // plane).astype(jnp.int32).reshape(1)
    row_count = steps * step_rows
    gate_lanes = -(-2 * row_count // 128) * 128
    smem = pl.BlockSpec(memory_space=pltpu.SMEM)

    packed, gates_trained, rows_trained = pl.pallas_call(
        lambda *refs: pack_kernel(steps, capacity, depth, *refs),
        out_shape=(
            pltpu.HBM((slots, hidden_width + gate_lanes), BF16),
            jax.ShapeDtypeStruct((2 * steps * step_rows, pair_slots), BF16),
            jax.ShapeDtypeStruct((pair_slots, hidden_width), BF16),
        ),
        in_specs=[smem] + vmem(3),
        out_specs=tuple(vmem(3)),
        compiler_params=PARAMS,
    )(
        placement,
        *in_hbm(
            routing.reshape(steps * step_rows, topk),
            gate_weight.reshape(steps * step_rows, topk),
            decode_hidden.reshape(entries, hidden_width),
        ),
    )
    hidden_other, cotangent_other = flip(learn_hidden, 1), flip(learn_cotangent, 1)
    same_core = [
        [z * plane + chip * 2 + core for chip in range(chips) for z in range(depth)]
        for core in range(2)
    ]
    received = lax.all_to_all(
        after(packed, hidden_other, cotangent_other).reshape(
            experts, pair_slots, hidden_width + gate_lanes
        ),
        "dp",
        split_axis=0,
        concat_axis=0,
        tiled=True,
        axis_index_groups=same_core,
    ).reshape(slots, hidden_width + gate_lanes)

    highs = devices // 16
    part = jax.ShapeDtypeStruct((highs, blocks, side, side), BF16)
    parts = pl.pallas_call(
        gradient_kernel,
        out_shape=(pltpu.HBM(part.shape, BF16),) * 8,
        in_specs=[smem] + vmem(4),
        out_specs=tuple(vmem(8)),
        scratch_shapes=[
            pltpu.VMEM((hidden_width, 2 * tokens), BF16),
            pltpu.VMEM((2 * tokens, columns), BF16),
        ],
        compiler_params=PARAMS,
    )(
        device_ref,
        *in_hbm(after(learn_hidden, packed), hidden_other, learn_cotangent, cotangent_other),
    )
    both_a, first_a, second_a, stay_a, both_b, first_b, second_b, stay_b = parts
    both_a, both_b = flip(both_a, 2), flip(both_b, 4)
    first_a, first_b = flip(first_a, 2), flip(first_b, 4)
    weights_other = flip(after(resident_weight, packed, hidden_other, cotangent_other), 1)
    scales_other = flip(resident_scale, 1)
    second_a = after(second_a, weights_other)
    second_a, second_b = pl.pallas_call(
        first_sum_kernel,
        out_shape=(pltpu.HBM(part.shape, BF16),) * 2,
        in_specs=vmem(4),
        out_specs=tuple(vmem(2)),
        compiler_params=PARAMS,
    )(both_a, *in_hbm(second_a), both_b, *in_hbm(second_b))
    sums = second_a, second_b
    second_a, second_b = flip(second_a, 4), flip(second_b, 2)

    plane_slots = depth * pair_slots
    sent_shape = (chips, plane_slots + pair_slots, columns + gate_lanes)

    def expert_sum(rows):
        wide = 512
        weight_spec = pl.BlockSpec((half, wide), lambda i, core: (0, i))
        scale_spec = pl.BlockSpec((row_blocks // 2, 1, wide), lambda i, core: (0, 0, i))
        return pl.pallas_call(
            expert_kernel,
            out_shape=pltpu.HBM(sent_shape, BF16),
            grid_spec=pltpu.PrefetchScalarGridSpec(
                num_scalar_prefetch=1,
                grid=(columns // wide,),
                in_specs=[
                    pl.BlockSpec((slots, hidden_width + gate_lanes), lambda i, core: (0, 0)),
                    pl.BlockSpec((pair_slots, hidden_width), lambda i, core: (0, 0)),
                    weight_spec,
                    weight_spec,
                    scale_spec,
                    scale_spec,
                ],
                out_specs=pl.BlockSpec(sent_shape, lambda i, core: (0, 0, 0)),
            ),
            compiler_params=PARAMS,
        )(
            bit(0).astype(jnp.int32).reshape(1),
            rows,
            rows_trained,
            resident_weight,
            weights_other,
            *(
                jnp.repeat(scales, side, axis=1)[:, None, :]
                for scales in (resident_scale, scales_other)
            ),
        )

    block_shape = (blocks, side, side)
    if highs == 2:
        expert_out = expert_sum(after(received, sums, first_a, first_b))
        parts = stay_a, first_a, second_a, stay_b, first_b, second_b
        high = (device // 8).astype(jnp.int32).reshape(1)
        piece = pl.BlockSpec((1,) + block_shape, lambda i, far: (far[0] % 2, 0, 0, 0))
        far = pl.pallas_call(
            far_sum_kernel,
            out_shape=jax.ShapeDtypeStruct(block_shape, BF16),
            grid_spec=pltpu.PrefetchScalarGridSpec(
                num_scalar_prefetch=1,
                grid=(1,),
                in_specs=[piece] * 6,
                out_specs=pl.BlockSpec(block_shape, lambda i, far: (0, 0, 0)),
            ),
            compiler_params=PARAMS,
        )(high ^ 3, *parts)
        expert_out = after(expert_out, far)
        near, across, own = pl.pallas_call(
            second_sum_kernel,
            out_shape=(
                jax.ShapeDtypeStruct(block_shape, BF16),
                jax.ShapeDtypeStruct(block_shape, F32),
                jax.ShapeDtypeStruct(block_shape, F32),
            ),
            in_specs=[smem] + vmem(6),
            out_specs=tuple(vmem(3)),
            scratch_shapes=[pltpu.VMEM((4,) + block_shape, F32)],
            compiler_params=PARAMS,
        )(after(high, far), *parts)
        far, near = flip(far, 8), flip(near, 8)
        across = pl.pallas_call(
            third_sum_kernel,
            out_shape=jax.ShapeDtypeStruct(block_shape, BF16),
            in_specs=vmem(2),
            out_specs=vmem(1)[0],
            compiler_params=PARAMS,
        )(far, across)
        gradient = [own, near, flip(across, 16)]
    else:
        expert_out = expert_sum(received)
        sums = [
            sum(piece.astype(F32) for piece in pieces)
            for pieces in ((stay_a, first_a, second_a), (stay_b, first_b, second_b))
        ]
        total = jnp.concatenate(sums, axis=0)
        number = 3
        while total.shape[0] > 1:
            split = total.reshape((-1, 2) + block_shape)
            sent = pick(split, 1 - bit(number), 1).astype(BF16)
            total = pick(split, bit(number), 1) + flip(sent, 2**number).astype(F32)
            number += 1
        gradient = [total[0]]
    new_master, fresh = pl.pallas_call(
        update_kernel,
        out_shape=(
            jax.ShapeDtypeStruct(block_shape, F32),
            jax.ShapeDtypeStruct(block_shape, BF16),
        ),
        in_specs=vmem(3 + len(gradient)),
        out_specs=tuple(vmem(2)),
        compiler_params=PARAMS,
    )(master, moment_first, moment_second, *gradient)

    same_core = [
        [z * plane + chip * 2 + core for chip in range(chips)]
        for z in range(depth)
        for core in range(2)
    ]
    returned = lax.all_to_all(
        expert_out, "dp", split_axis=0, concat_axis=0, tiled=True, axis_index_groups=same_core
    )
    rows_trained = returned[:, plane_slots:, :hidden_width]
    row_shape = (row_count, columns)
    mixed, across_rows, sent_rows = pl.pallas_call(
        lambda *refs: mix_kernel(depth, plane_slots, *refs),
        out_shape=(
            jax.ShapeDtypeStruct(row_shape, F32),
            jax.ShapeDtypeStruct(row_shape, F32),
            jax.ShapeDtypeStruct((2,) + row_shape, BF16),
        ),
        in_specs=[smem] + vmem(1),
        out_specs=tuple(vmem(3)),
        compiler_params=PARAMS,
    )(floor_ref, after(returned, fresh))
    sent_rows = flip(sent_rows, plane)
    across_rows, mixed_near = pl.pallas_call(
        mix_sum_kernel,
        out_shape=(
            jax.ShapeDtypeStruct(row_shape, BF16),
            jax.ShapeDtypeStruct(row_shape, F32),
        ),
        in_specs=vmem(3),
        out_specs=tuple(vmem(2)),
        compiler_params=PARAMS,
    )(sent_rows, across_rows, mixed)
    across_rows = flip(across_rows, 2 * plane)

    held = {0: fresh}
    mask = depth // 2
    while mask:
        for key in list(held):
            held[key | mask] = flip(held[key], mask * plane)
        mask //= 2
    blocks_held = [held[z] for z in range(depth)]
    blocks_held += [flip(block, 1) for block in blocks_held]
    chip_ref = (device % plane // 2).astype(jnp.int32).reshape(1)
    trained = pl.pallas_call(
        lambda device_ref, *refs: trained_kernel(device_ref, plane, depth, column_blocks, *refs),
        out_shape=(jax.ShapeDtypeStruct((pair_slots, 2 * blocks * side), BF16),) * chips,
        in_specs=[smem] + vmem(1 + 2 * depth),
        out_specs=tuple(vmem(chips)),
        compiler_params=PARAMS,
    )(device_ref, after(rows_trained, mixed), *blocks_held)
    trained = [trained[0]] + [flip(trained[turn], 2 * turn) for turn in range(1, chips)]
    decoded = pl.pallas_call(
        lambda chip_ref, *refs: combine_kernel(chip_ref, chips, side, *refs),
        out_shape=jax.ShapeDtypeStruct((row_count, columns), BF16),
        in_specs=[smem] + vmem(3 + chips),
        out_specs=vmem(1)[0],
        scratch_shapes=[pltpu.VMEM((pair_slots, columns), F32)],
        compiler_params=PARAMS,
    )(chip_ref, gates_trained, mixed_near, across_rows, *trained)
    return (decoded.reshape(steps, step_rows, columns), new_master)


def solution(mesh):
    return jax.shard_map(
        local,
        mesh=mesh,
        in_specs=(
            P(("groups", "dp"), None),
            P(("groups", "dp"), None),
            P("dp", None, None),
            P("dp", None, None),
            P("dp", None, None),
            P("dp", None),
            P("dp", None),
            P(),
            P(None, ("groups", "dp"), None, None),
            P(None, ("groups", "dp"), None),
            P(None, ("groups", "dp"), None),
        ),
        out_specs=(P(None, ("groups", "dp"), None), P(("groups", "dp"), None, None)),
        check_vma=False,
    )
```

```python
import jax
import jax.numpy as jnp
from jax import lax
from jax.experimental import pallas as pl
from jax.experimental.pallas import tpu as pltpu
from jax.sharding import PartitionSpec as P

learn_rate = 0.05
beta_first = 0.9
beta_second = 0.95
correct_first = 1.0 - 0.9**10
correct_second = 1.0 - 0.95**10
decay_rate = 0.1
adam_epsilon = 1e-08
quant_range = 448.0

F32 = jnp.float32
BF16 = jnp.bfloat16
PARAMS = pltpu.CompilerParams(vmem_limit_bytes=16 * 2**20)


def optimizer(gradient, master, moment_first, moment_second):
    first_moment = beta_first * moment_first + (1.0 - beta_first) * gradient
    second_moment = beta_second * moment_second + (1.0 - beta_second) * gradient * gradient
    update = (
        first_moment / correct_first / (jnp.sqrt(second_moment / correct_second) + adam_epsilon)
    )
    return master - learn_rate * (update + decay_rate * master)


def update_kernel(master, moment_first, moment_second, *rest):
    parts, new_master, fresh = rest[:-2], rest[-2], rest[-1]
    for block in range(master.shape[0]):
        gradient = parts[0][block].astype(F32)
        for part in parts[1:]:
            gradient = gradient + part[block].astype(F32)
        weights = optimizer(gradient, master[block], moment_first[block], moment_second[block])
        new_master[block] = weights
        largest = jnp.max(jnp.abs(weights), axis=(0, 1), keepdims=True)
        scale = (largest + 1e-06) / quant_range
        quantized = (weights / scale).astype(BF16)
        fresh[block] = (quantized.astype(F32) * scale).astype(BF16)


def in_hbm(*arrays):
    return [pltpu.with_memory_space_constraint(array, pltpu.HBM) for array in arrays]


def vmem(count):
    return [pl.BlockSpec(memory_space=pltpu.VMEM)] * count


def part_of(index, size):
    if size & (size - 1) == 0:
        return lax.shift_right_logical(index, jnp.full_like(index, size.bit_length() - 1))
    return index // size


def pack_kernel(
    steps,
    capacity,
    depth,
    placement,
    routing,
    gate_weight,
    hidden_hbm,
    packed_hbm,
    gates_trained,
    rows_trained,
    hidden,
    packed,
    hidden_sem,
    packed_sems,
):
    arriving = pltpu.make_async_copy(hidden_hbm, hidden, hidden_sem)
    arriving.start()
    rows, topk = routing.shape
    entries = rows * topk
    step_entries = entries // steps
    experts = placement.shape[0]
    chips = experts // depth
    pair_slots = steps * capacity

    def iota(shape, axis):
        return lax.broadcasted_iota(jnp.int32, shape, axis)

    def ones(mask):
        return jnp.where(mask, 1.0, 0.0).astype(BF16)

    entry = iota((1, entries), 1)
    entry_row = part_of(entry, topk)
    spread = ones(entry - entry_row * topk == iota((topk, entries), 0))
    mine = entry_row == iota((rows, entries), 0)

    def along(values):
        return jnp.where(mine, jnp.dot(values, spread, preferred_element_type=F32), 0.0)

    routed = jnp.sum(along(routing[...].astype(F32).astype(BF16)), axis=0, keepdims=True)
    routed = routed.astype(jnp.int32)
    named = ones(iota((experts, entries), 0) == routed)
    same = lax.dot_general(named, named, (((0,), (0,)), ((), ())), preferred_element_type=F32)
    lane, line = iota((1, entries), 1), iota((entries, 1), 0)
    earlier = (part_of(line, topk) < part_of(lane, topk)) & (
        part_of(line, step_entries) == part_of(lane, step_entries)
    )
    place = jnp.sum(jnp.where(earlier, same, 0.0), axis=0, keepdims=True).astype(jnp.int32)
    pair = jnp.zeros_like(routed)
    for expert in range(experts):
        pair = jnp.where(routed == expert, placement[expert], pair)
    step_slot = part_of(entry, step_entries) * capacity + place
    floor = part_of(pair, chips)
    slot = ((pair - floor * chips) * depth + floor) * pair_slots + step_slot
    slots = experts * pair_slots
    slot_line = lax.broadcasted_iota(jnp.int32, (slots, entries), 0)
    onehot = jnp.where(slot_line == slot, 1.0, 0.0).astype(BF16)
    width = hidden.shape[1]
    arriving.wait()
    leaving = []

    def leave(at):
        copy = pltpu.make_async_copy(
            packed.at[:, at], packed_hbm.at[:, at], packed_sems.at[len(leaving)]
        )
        copy.start()
        leaving.append(copy)

    wide = width // 3
    for column in range(0, width, wide):
        at = slice(column, column + wide)
        packed[:, at] = jnp.dot(onehot, hidden[:, at], preferred_element_type=F32).astype(BF16)
        leave(pl.ds(column, wide))
    onehot_trained = ones((iota((pair_slots, entries), 0) == step_slot) & (routed == 0))
    rows_trained[...] = jnp.dot(
        onehot_trained, hidden[...], preferred_element_type=F32
    ).astype(BF16)
    weight = gate_weight[...]
    high = weight.astype(BF16)
    rest = (weight - high.astype(F32)).astype(BF16)
    both = jnp.concatenate([along(high), along(rest)], axis=0).astype(BF16)
    over_entries = (((1,), (1,)), ((), ()))
    gates_trained[...] = lax.dot_general(
        both, onehot_trained, over_entries, preferred_element_type=F32
    ).astype(BF16)
    counted = jnp.where(routed == 0, 0.0, both.astype(F32)).astype(BF16)
    unused = jnp.zeros((packed.shape[1] - width - 2 * rows, entries), BF16)
    packed[:, width:] = lax.dot_general(
        onehot,
        jnp.concatenate([counted, unused], axis=0),
        over_entries,
        preferred_element_type=F32,
    ).astype(BF16)
    leave(pl.ds(width, packed.shape[1] - width))
    for copy in leaving:
        copy.wait()


def gradient_kernel(
    device_ref, hidden_own, hidden_other, cotangent_own, cotangent_other, *rest
):
    outs, hidden_across, cotangent = rest[:8], rest[8], rest[9]
    device = device_ref[0]
    tokens = hidden_own.shape[0]
    hidden_across[:, :tokens] = hidden_own[...].T
    hidden_across[:, tokens:] = hidden_other[...].T
    cotangent[:tokens] = cotangent_own[...]
    cotangent[tokens:] = cotangent_other[...]
    highs, blocks, side, _ = outs[0].shape
    column_blocks = cotangent.shape[1] // side
    wide = 2 if blocks % 2 == 0 else 1
    core = device % 2
    bit_x = device // 2 % 2
    bit_y = device // 4 % 2
    for part in range(4):
        for half in range(2):
            first, second = part < 2, part % 2 == 0
            over_x, over_y = (first, second) if half == 0 else (second, first)
            x = 1 - bit_x if over_x else bit_x
            y = 1 - bit_y if over_y else bit_y
            out = outs[4 * half + part]
            for high in range(highs):
                dest = (((high + half * highs) * 2 + y) * 2 + x) * 2 + core
                for at in range(0, blocks, wide):
                    block = dest * blocks + at
                    row = pl.multiple_of(block // column_blocks * side, side)
                    column = pl.multiple_of(block % column_blocks * side, side)
                    product = jnp.dot(
                        hidden_across[pl.ds(row, side), :],
                        cotangent[:, pl.ds(column, wide * side)],
                        preferred_element_type=F32,
                    ).astype(out.dtype)
                    for piece in range(wide):
                        out[high, at + piece] = product[:, piece * side : (piece + 1) * side]


def first_sum_kernel(arrived_a, held_a, arrived_b, held_b, out_a, out_b):
    out_a[...] = (arrived_a[...].astype(F32) + held_a[...].astype(F32)).astype(BF16)
    out_b[...] = (arrived_b[...].astype(F32) + held_b[...].astype(F32)).astype(BF16)


def far_sum_kernel(far_ref, *rest):
    parts, out = rest[:6], rest[6]
    for half in range(2):

        @pl.when(far_ref[0] // 2 == half)
        def _(pieces=parts[3 * half : 3 * half + 3]):
            one, two, three = (piece[0].astype(F32) for piece in pieces)
            out[...] = (one + two + three).astype(out.dtype)


def second_sum_kernel(floor_ref, *rest):
    parts, outs, total = rest[:6], rest[6:9], rest[9]
    highs = parts[0].shape[0]
    for half in range(2):
        one, two, three = parts[3 * half : 3 * half + 3]
        total[half * highs : (half + 1) * highs] = (
            one[...].astype(F32) + two[...].astype(F32) + three[...].astype(F32)
        )
    for flip, out in zip((1, 2, 0), outs, strict=True):
        out[...] = total[floor_ref[0] ^ flip].astype(out.dtype)


def third_sum_kernel(arrived, held, out):
    out[...] = (arrived[...].astype(F32) + held[...].astype(F32)).astype(BF16)


def expert_partial(rows, weights, scales):
    blocks, side = scales.shape[0], weights.shape[0] // scales.shape[0]
    scaled = [
        (weights[at * side : (at + 1) * side].astype(F32) * scales[at]).astype(BF16)
        for at in range(blocks)
    ]
    scaled = jnp.concatenate(scaled, axis=0)
    return jnp.dot(rows, scaled, preferred_element_type=F32).astype(BF16)


def expert_kernel(
    core_ref, rows, rows_trained, weights, weights_other, scales, scales_other, out
):
    half, wide = weights.shape
    step = pl.program_id(0)
    total = 0.0
    for core, kept, scale in (
        (core_ref[0], weights, scales),
        (1 - core_ref[0], weights_other, scales_other),
    ):
        at = pl.ds(pl.multiple_of(core * half, half), half)
        total = total + expert_partial(rows[:, at], kept, scale).astype(F32)
    chips = out.shape[0]
    count = rows.shape[0] // chips
    for chip in range(chips):
        out[chip, :count, pl.ds(pl.multiple_of(step * wide, wide), wide)] = total[
            chip * count : (chip + 1) * count
        ].astype(out.dtype)

    @pl.when(step == 0)
    def _():
        columns = wide * pl.num_programs(0)
        for chip in range(chips):
            out[chip, :count, columns:] = rows[chip * count : (chip + 1) * count, 2 * half :]
            out[chip, count:, : 2 * half] = rows_trained[...]
            out[chip, count:, 2 * half :] = jnp.zeros(
                (out.shape[1] - count, out.shape[2] - 2 * half), out.dtype
            )


def trained_kernel(device_ref, plane, depth, column_blocks, rows, *rest):
    weights, outs = rest[: 2 * depth], rest[2 * depth :]
    device = device_ref[0]
    blocks, side, _ = weights[0].shape
    floor = device // plane
    chip = device % plane // 2
    chips, count, _ = rows.shape
    for core in range(2):
        number = device % 2 ^ core
        for at in range(blocks):
            total = jnp.zeros((chips * count, side), F32)
            for flip in range(depth):
                block = (floor ^ flip) * plane * blocks + (chip * 2 + number) * blocks + at
                start = pl.multiple_of(block // column_blocks * side, side)
                part = jnp.concatenate(
                    [rows[chip ^ turn, :, pl.ds(start, side)] for turn in range(chips)], axis=0
                )
                total = total + jnp.dot(
                    part, weights[core * depth + flip][at], preferred_element_type=F32
                )
            column = pl.ds(pl.multiple_of((number * blocks + at) * side, side), side)
            for turn in range(chips):
                outs[turn][:, column] = total[turn * count : (turn + 1) * count].astype(BF16)


def mix_kernel(depth, plane_slots, floor_ref, returned, own, across, sent):
    count, columns = own.shape
    outs = own, sent.at[0], across, sent.at[1]

    def of_chips(at):
        return jnp.concatenate(
            [returned[chip, :plane_slots, at] for chip in range(returned.shape[0])], axis=0
        )

    gates = of_chips(slice(columns, None)).astype(F32)
    share = plane_slots // depth
    pieces = [gates[top : top + share] for top in range(0, gates.shape[0], share)]
    mine = []
    for flip in range(depth):
        there = floor_ref[0] ^ flip
        kept = [jnp.where(there == at % depth, piece, 0.0) for at, piece in enumerate(pieces)]
        mine.append(jnp.concatenate(kept, axis=0).astype(BF16))
    wide = 512
    for column in range(0, columns, wide):
        at = slice(column, column + wide)
        rows = of_chips(at)
        for flip, out in enumerate(outs):
            mixed = lax.dot_general(
                mine[flip], rows, (((0,), (0,)), ((), ())), preferred_element_type=F32
            )
            out[:, at] = (mixed[:count] + mixed[count : 2 * count]).astype(out.dtype)


def mix_sum_kernel(arrived, across, own, out_across, out_own):
    out_across[...] = (arrived[1].astype(F32) + across[...]).astype(BF16)
    out_own[...] = arrived[0].astype(F32) + own[...]


def combine_kernel(chip_ref, chips, side, gates_trained, near, across, *rest):
    trained, out, fresh = rest[:chips], rest[chips], rest[chips + 1]
    columns = out.shape[1]
    blocks = trained[0].shape[1] // side
    count = out.shape[0]
    fresh[...] = jnp.zeros_like(fresh)
    for turn in range(chips):
        for at in range(blocks):
            number = ((chip_ref[0] ^ turn) * blocks + at) % (columns // side)
            column = pl.ds(pl.multiple_of(number * side, side), side)
            fresh[:, column] += trained[turn][:, at * side : (at + 1) * side].astype(F32)
    wide = 512
    for column in range(0, columns, wide):
        at = slice(column, column + wide)
        both = jnp.dot(gates_trained[...], fresh[:, at].astype(BF16), preferred_element_type=F32)
        total = both[:count] + both[count:] + near[:, at] + across[:, at].astype(F32)
        out[:, at] = total.astype(out.dtype)


def local(
    learn_hidden,
    learn_cotangent,
    master,
    moment_first,
    moment_second,
    resident_weight,
    resident_scale,
    placement,
    decode_hidden,
    routing,
    gate_weight,
):
    devices = lax.axis_size("dp")
    device = lax.axis_index("dp")
    device_ref = device.astype(jnp.int32).reshape(1)
    blocks, side = master.shape[:2]
    hidden_width = learn_hidden.shape[1]
    columns = learn_cotangent.shape[1]
    row_blocks = hidden_width // side
    column_blocks = columns // side
    tokens = learn_hidden.shape[0]
    steps, step_rows, topk = routing.shape
    experts = placement.shape[0]
    capacity = min(step_rows, step_rows * topk // experts + 2)
    entries = steps * step_rows * topk
    pair_slots = steps * capacity
    slots = experts * pair_slots
    half = hidden_width // 2

    def flip(array, mask):
        return lax.ppermute(array, "dp", [(i, i ^ mask) for i in range(devices)])

    def bit(number):
        return device // 2**number % 2

    def after(array, *others):
        return lax.optimization_barrier((array, others))[0]

    def pick(array, index, axis):
        return lax.dynamic_index_in_dim(array, index, axis, keepdims=False)

    plane = 1
    while plane * blocks % column_blocks:
        plane *= 2
    depth = devices // plane
    chips = plane // 2
    floor_ref = (device // plane).astype(jnp.int32).reshape(1)
    row_count = steps * step_rows
    gate_lanes = -(-2 * row_count // 128) * 128
    smem = pl.BlockSpec(memory_space=pltpu.SMEM)
    hbm = pl.BlockSpec(memory_space=pl.ANY)

    packed, gates_trained, rows_trained = pl.pallas_call(
        lambda *refs: pack_kernel(steps, capacity, depth, *refs),
        out_shape=(
            pltpu.HBM((slots, hidden_width + gate_lanes), BF16),
            jax.ShapeDtypeStruct((2 * steps * step_rows, pair_slots), BF16),
            jax.ShapeDtypeStruct((pair_slots, hidden_width), BF16),
        ),
        in_specs=[smem] + vmem(2) + [hbm],
        out_specs=(hbm, *vmem(2)),
        scratch_shapes=[
            pltpu.VMEM((entries, hidden_width), BF16),
            pltpu.VMEM((slots, hidden_width + gate_lanes), BF16),
            pltpu.SemaphoreType.DMA,
            pltpu.SemaphoreType.DMA((4,)),
        ],
        compiler_params=PARAMS,
    )(
        *in_hbm(
            placement,
            routing.reshape(steps * step_rows, topk),
            gate_weight.reshape(steps * step_rows, topk),
            decode_hidden.reshape(entries, hidden_width),
        ),
    )
    hidden_other, cotangent_other = flip(learn_hidden, 1), flip(learn_cotangent, 1)
    same_core = [
        [z * plane + chip * 2 + core for chip in range(chips) for z in range(depth)]
        for core in range(2)
    ]
    received = lax.all_to_all(
        after(packed, hidden_other, cotangent_other).reshape(
            experts, pair_slots, hidden_width + gate_lanes
        ),
        "dp",
        split_axis=0,
        concat_axis=0,
        tiled=True,
        axis_index_groups=same_core,
    ).reshape(slots, hidden_width + gate_lanes)

    highs = devices // 16
    part = jax.ShapeDtypeStruct((highs, blocks, side, side), BF16)
    parts = pl.pallas_call(
        gradient_kernel,
        out_shape=(pltpu.HBM(part.shape, BF16),) * 8,
        in_specs=[smem] + vmem(4),
        out_specs=tuple(vmem(8)),
        scratch_shapes=[
            pltpu.VMEM((hidden_width, 2 * tokens), BF16),
            pltpu.VMEM((2 * tokens, columns), BF16),
        ],
        compiler_params=PARAMS,
    )(
        device_ref,
        *in_hbm(after(learn_hidden, packed), hidden_other, learn_cotangent, cotangent_other),
    )
    both_a, first_a, second_a, stay_a, both_b, first_b, second_b, stay_b = parts
    both_a, both_b = flip(both_a, 2), flip(both_b, 4)
    first_a, first_b = flip(first_a, 2), flip(first_b, 4)
    weights_other = flip(after(resident_weight, packed, hidden_other, cotangent_other), 1)
    scales_other = flip(resident_scale, 1)
    second_a = after(second_a, weights_other)
    second_a, second_b = pl.pallas_call(
        first_sum_kernel,
        out_shape=(pltpu.HBM(part.shape, BF16),) * 2,
        in_specs=vmem(4),
        out_specs=tuple(vmem(2)),
        compiler_params=PARAMS,
    )(both_a, *in_hbm(second_a), both_b, *in_hbm(second_b))
    sums = second_a, second_b
    second_a, second_b = flip(second_a, 4), flip(second_b, 2)

    plane_slots = depth * pair_slots
    sent_shape = (chips, plane_slots + pair_slots, columns + gate_lanes)

    def expert_sum(rows):
        wide = 512
        weight_spec = pl.BlockSpec((half, wide), lambda i, core: (0, i))
        scale_spec = pl.BlockSpec((row_blocks // 2, 1, wide), lambda i, core: (0, 0, i))
        return pl.pallas_call(
            expert_kernel,
            out_shape=pltpu.HBM(sent_shape, BF16),
            grid_spec=pltpu.PrefetchScalarGridSpec(
                num_scalar_prefetch=1,
                grid=(columns // wide,),
                in_specs=[
                    pl.BlockSpec((slots, hidden_width + gate_lanes), lambda i, core: (0, 0)),
                    pl.BlockSpec((pair_slots, hidden_width), lambda i, core: (0, 0)),
                    weight_spec,
                    weight_spec,
                    scale_spec,
                    scale_spec,
                ],
                out_specs=pl.BlockSpec(sent_shape, lambda i, core: (0, 0, 0)),
            ),
            compiler_params=PARAMS,
        )(
            bit(0).astype(jnp.int32).reshape(1),
            rows,
            rows_trained,
            resident_weight,
            weights_other,
            *(
                jnp.repeat(scales, side, axis=1)[:, None, :]
                for scales in (resident_scale, scales_other)
            ),
        )

    block_shape = (blocks, side, side)
    if highs == 2:
        expert_out = expert_sum(after(received, sums, first_a, first_b))
        parts = stay_a, first_a, second_a, stay_b, first_b, second_b
        high = (device // 8).astype(jnp.int32).reshape(1)
        piece = pl.BlockSpec((1,) + block_shape, lambda i, far: (far[0] % 2, 0, 0, 0))
        far = pl.pallas_call(
            far_sum_kernel,
            out_shape=jax.ShapeDtypeStruct(block_shape, BF16),
            grid_spec=pltpu.PrefetchScalarGridSpec(
                num_scalar_prefetch=1,
                grid=(1,),
                in_specs=[piece] * 6,
                out_specs=pl.BlockSpec(block_shape, lambda i, far: (0, 0, 0)),
            ),
            compiler_params=PARAMS,
        )(high ^ 3, *parts)
        expert_out = after(expert_out, far)
        near, across, own = pl.pallas_call(
            second_sum_kernel,
            out_shape=(
                jax.ShapeDtypeStruct(block_shape, BF16),
                jax.ShapeDtypeStruct(block_shape, F32),
                jax.ShapeDtypeStruct(block_shape, F32),
            ),
            in_specs=[smem] + vmem(6),
            out_specs=tuple(vmem(3)),
            scratch_shapes=[pltpu.VMEM((4,) + block_shape, F32)],
            compiler_params=PARAMS,
        )(after(high, far), *parts)
        far, near = flip(far, 8), flip(near, 8)
        across = pl.pallas_call(
            third_sum_kernel,
            out_shape=jax.ShapeDtypeStruct(block_shape, BF16),
            in_specs=vmem(2),
            out_specs=vmem(1)[0],
            compiler_params=PARAMS,
        )(far, across)
        gradient = [own, near, flip(across, 16)]
    else:
        expert_out = expert_sum(received)
        sums = [
            sum(piece.astype(F32) for piece in pieces)
            for pieces in ((stay_a, first_a, second_a), (stay_b, first_b, second_b))
        ]
        total = jnp.concatenate(sums, axis=0)
        number = 3
        while total.shape[0] > 1:
            split = total.reshape((-1, 2) + block_shape)
            sent = pick(split, 1 - bit(number), 1).astype(BF16)
            total = pick(split, bit(number), 1) + flip(sent, 2**number).astype(F32)
            number += 1
        gradient = [total[0]]
    new_master, fresh = pl.pallas_call(
        update_kernel,
        out_shape=(
            jax.ShapeDtypeStruct(block_shape, F32),
            jax.ShapeDtypeStruct(block_shape, BF16),
        ),
        in_specs=vmem(3 + len(gradient)),
        out_specs=tuple(vmem(2)),
        compiler_params=PARAMS,
    )(master, moment_first, moment_second, *gradient)

    same_core = [
        [z * plane + chip * 2 + core for chip in range(chips)]
        for z in range(depth)
        for core in range(2)
    ]
    returned = lax.all_to_all(
        expert_out, "dp", split_axis=0, concat_axis=0, tiled=True, axis_index_groups=same_core
    )
    rows_trained = returned[:, plane_slots:, :hidden_width]
    row_shape = (row_count, columns)
    mixed, across_rows, sent_rows = pl.pallas_call(
        lambda *refs: mix_kernel(depth, plane_slots, *refs),
        out_shape=(
            jax.ShapeDtypeStruct(row_shape, F32),
            jax.ShapeDtypeStruct(row_shape, F32),
            jax.ShapeDtypeStruct((2,) + row_shape, BF16),
        ),
        in_specs=[smem] + vmem(1),
        out_specs=tuple(vmem(3)),
        compiler_params=PARAMS,
    )(floor_ref, after(returned, fresh))
    sent_rows = flip(sent_rows, plane)
    across_rows, mixed_near = pl.pallas_call(
        mix_sum_kernel,
        out_shape=(
            jax.ShapeDtypeStruct(row_shape, BF16),
            jax.ShapeDtypeStruct(row_shape, F32),
        ),
        in_specs=vmem(3),
        out_specs=tuple(vmem(2)),
        compiler_params=PARAMS,
    )(sent_rows, across_rows, mixed)
    across_rows = flip(across_rows, 2 * plane)

    held = {0: fresh}
    mask = depth // 2
    while mask:
        for key in list(held):
            held[key | mask] = flip(held[key], mask * plane)
        mask //= 2
    blocks_held = [held[z] for z in range(depth)]
    blocks_held += [flip(after(block, held[depth // 2]), 1) for block in blocks_held]
    chip_ref = (device % plane // 2).astype(jnp.int32).reshape(1)
    trained = pl.pallas_call(
        lambda device_ref, *refs: trained_kernel(device_ref, plane, depth, column_blocks, *refs),
        out_shape=(jax.ShapeDtypeStruct((pair_slots, 2 * blocks * side), BF16),) * chips,
        in_specs=[smem] + vmem(1 + 2 * depth),
        out_specs=tuple(vmem(chips)),
        compiler_params=PARAMS,
    )(device_ref, after(rows_trained, mixed), *blocks_held)
    trained = [trained[0]] + [flip(trained[turn], 2 * turn) for turn in range(1, chips)]
    decoded = pl.pallas_call(
        lambda chip_ref, *refs: combine_kernel(chip_ref, chips, side, *refs),
        out_shape=jax.ShapeDtypeStruct((row_count, columns), BF16),
        in_specs=[smem] + vmem(3 + chips),
        out_specs=vmem(1)[0],
        scratch_shapes=[pltpu.VMEM((pair_slots, columns), F32)],
        compiler_params=PARAMS,
    )(chip_ref, gates_trained, mixed_near, across_rows, *trained)
    return (decoded.reshape(steps, step_rows, columns), new_master)


def solution(mesh):
    return jax.shard_map(
        local,
        mesh=mesh,
        in_specs=(
            P(("groups", "dp"), None),
            P(("groups", "dp"), None),
            P("dp", None, None),
            P("dp", None, None),
            P("dp", None, None),
            P("dp", None),
            P("dp", None),
            P(),
            P(None, ("groups", "dp"), None, None),
            P(None, ("groups", "dp"), None),
            P(None, ("groups", "dp"), None),
        ),
        out_specs=(P(None, ("groups", "dp"), None), P(("groups", "dp"), None, None)),
        check_vma=False,
    )
```

```python
import jax
import jax.numpy as jnp
from jax import lax
from jax.experimental import pallas as pl
from jax.experimental.pallas import tpu as pltpu
from jax.sharding import PartitionSpec as P

learn_rate = 0.05
beta_first = 0.9
beta_second = 0.95
correct_first = 1.0 - 0.9**10
correct_second = 1.0 - 0.95**10
decay_rate = 0.1
adam_epsilon = 1e-08
quant_range = 448.0

F32 = jnp.float32
BF16 = jnp.bfloat16
PARAMS = pltpu.CompilerParams(vmem_limit_bytes=16 * 2**20)


def optimizer(gradient, master, moment_first, moment_second):
    first_moment = beta_first * moment_first + (1.0 - beta_first) * gradient
    second_moment = beta_second * moment_second + (1.0 - beta_second) * gradient * gradient
    update = (
        first_moment / correct_first / (jnp.sqrt(second_moment / correct_second) + adam_epsilon)
    )
    return master - learn_rate * (update + decay_rate * master)


def update_kernel(master, moment_first, moment_second, *rest):
    parts, new_master, fresh = rest[:-2], rest[-2], rest[-1]
    for block in range(master.shape[0]):
        gradient = parts[0][block].astype(F32)
        for part in parts[1:]:
            gradient = gradient + part[block].astype(F32)
        weights = optimizer(gradient, master[block], moment_first[block], moment_second[block])
        new_master[block] = weights
        largest = jnp.max(jnp.abs(weights), axis=(0, 1), keepdims=True)
        scale = (largest + 1e-06) / quant_range
        quantized = (weights / scale).astype(BF16)
        fresh[block] = (quantized.astype(F32) * scale).astype(BF16)


def in_hbm(*arrays):
    return [pltpu.with_memory_space_constraint(array, pltpu.HBM) for array in arrays]


def vmem(count):
    return [pl.BlockSpec(memory_space=pltpu.VMEM)] * count


def part_of(index, size):
    if size & (size - 1) == 0:
        return lax.shift_right_logical(index, jnp.full_like(index, size.bit_length() - 1))
    return index // size


def pack_kernel(
    steps,
    capacity,
    depth,
    placement,
    routing,
    gate_weight,
    hidden_hbm,
    packed_hbm,
    gates_trained,
    rows_trained,
    hidden,
    packed,
    hidden_sem,
    packed_sems,
):
    arriving = pltpu.make_async_copy(hidden_hbm, hidden, hidden_sem)
    arriving.start()
    rows, topk = routing.shape
    entries = rows * topk
    step_entries = entries // steps
    experts = placement.shape[0]
    chips = experts // depth
    pair_slots = steps * capacity

    def iota(shape, axis):
        return lax.broadcasted_iota(jnp.int32, shape, axis)

    def ones(mask):
        return jnp.where(mask, 1.0, 0.0).astype(BF16)

    entry = iota((1, entries), 1)
    entry_row = part_of(entry, topk)
    spread = ones(entry - entry_row * topk == iota((topk, entries), 0))
    mine = entry_row == iota((rows, entries), 0)

    def along(values):
        return jnp.where(mine, jnp.dot(values, spread, preferred_element_type=F32), 0.0)

    routed = jnp.sum(along(routing[...].astype(F32).astype(BF16)), axis=0, keepdims=True)
    routed = routed.astype(jnp.int32)
    named = ones(iota((experts, entries), 0) == routed)
    same = lax.dot_general(named, named, (((0,), (0,)), ((), ())), preferred_element_type=F32)
    lane, line = iota((1, entries), 1), iota((entries, 1), 0)
    earlier = (part_of(line, topk) < part_of(lane, topk)) & (
        part_of(line, step_entries) == part_of(lane, step_entries)
    )
    place = jnp.sum(jnp.where(earlier, same, 0.0), axis=0, keepdims=True).astype(jnp.int32)
    pair = jnp.zeros_like(routed)
    for expert in range(experts):
        pair = jnp.where(routed == expert, placement[expert], pair)
    step_slot = part_of(entry, step_entries) * capacity + place
    floor = part_of(pair, chips)
    slot = ((pair - floor * chips) * depth + floor) * pair_slots + step_slot
    slots = experts * pair_slots
    slot_line = lax.broadcasted_iota(jnp.int32, (slots, entries), 0)
    onehot = jnp.where(slot_line == slot, 1.0, 0.0).astype(BF16)
    width = hidden.shape[1]
    arriving.wait()
    leaving = []

    def leave(at):
        copy = pltpu.make_async_copy(
            packed.at[:, at], packed_hbm.at[:, at], packed_sems.at[len(leaving)]
        )
        copy.start()
        leaving.append(copy)

    wide = width // 3
    for column in range(0, width, wide):
        at = slice(column, column + wide)
        packed[:, at] = jnp.dot(onehot, hidden[:, at], preferred_element_type=F32).astype(BF16)
        leave(pl.ds(column, wide))
    onehot_trained = ones((iota((pair_slots, entries), 0) == step_slot) & (routed == 0))
    rows_trained[...] = jnp.dot(
        onehot_trained, hidden[...], preferred_element_type=F32
    ).astype(BF16)
    weight = gate_weight[...]
    high = weight.astype(BF16)
    rest = (weight - high.astype(F32)).astype(BF16)
    both = jnp.concatenate([along(high), along(rest)], axis=0).astype(BF16)
    over_entries = (((1,), (1,)), ((), ()))
    gates_trained[...] = lax.dot_general(
        both, onehot_trained, over_entries, preferred_element_type=F32
    ).astype(BF16)
    counted = jnp.where(routed == 0, 0.0, both.astype(F32)).astype(BF16)
    unused = jnp.zeros((packed.shape[1] - width - 2 * rows, entries), BF16)
    packed[:, width:] = lax.dot_general(
        onehot,
        jnp.concatenate([counted, unused], axis=0),
        over_entries,
        preferred_element_type=F32,
    ).astype(BF16)
    leave(pl.ds(width, packed.shape[1] - width))
    for copy in leaving:
        copy.wait()


def gradient_kernel(
    device_ref, hidden_own, hidden_other, cotangent_own, cotangent_other, *rest
):
    outs, hidden_across, cotangent = rest[:8], rest[8], rest[9]
    device = device_ref[0]
    tokens = hidden_own.shape[0]
    hidden_across[:, :tokens] = hidden_own[...].T
    hidden_across[:, tokens:] = hidden_other[...].T
    cotangent[:tokens] = cotangent_own[...]
    cotangent[tokens:] = cotangent_other[...]
    highs, blocks, side, _ = outs[0].shape
    column_blocks = cotangent.shape[1] // side
    wide = 2 if blocks % 2 == 0 else 1
    core = device % 2
    bit_x = device // 2 % 2
    bit_y = device // 4 % 2
    for part in range(4):
        for half in range(2):
            first, second = part < 2, part % 2 == 0
            over_x, over_y = (first, second) if half == 0 else (second, first)
            x = 1 - bit_x if over_x else bit_x
            y = 1 - bit_y if over_y else bit_y
            out = outs[4 * half + part]
            for high in range(highs):
                dest = (((high + half * highs) * 2 + y) * 2 + x) * 2 + core
                for at in range(0, blocks, wide):
                    block = dest * blocks + at
                    row = pl.multiple_of(block // column_blocks * side, side)
                    column = pl.multiple_of(block % column_blocks * side, side)
                    product = jnp.dot(
                        hidden_across[pl.ds(row, side), :],
                        cotangent[:, pl.ds(column, wide * side)],
                        preferred_element_type=F32,
                    ).astype(out.dtype)
                    for piece in range(wide):
                        out[high, at + piece] = product[:, piece * side : (piece + 1) * side]


def first_sum_kernel(arrived_a, held_a, arrived_b, held_b, out_a, out_b):
    out_a[...] = (arrived_a[...].astype(F32) + held_a[...].astype(F32)).astype(BF16)
    out_b[...] = (arrived_b[...].astype(F32) + held_b[...].astype(F32)).astype(BF16)


def far_sum_kernel(far_ref, *rest):
    parts, out = rest[:6], rest[6]
    for half in range(2):

        @pl.when(far_ref[0] // 2 == half)
        def _(pieces=parts[3 * half : 3 * half + 3]):
            one, two, three = (piece[0].astype(F32) for piece in pieces)
            out[...] = (one + two + three).astype(out.dtype)


def second_sum_kernel(floor_ref, *rest):
    parts, outs, total = rest[:6], rest[6:9], rest[9]
    highs = parts[0].shape[0]
    for half in range(2):
        one, two, three = parts[3 * half : 3 * half + 3]
        total[half * highs : (half + 1) * highs] = (
            one[...].astype(F32) + two[...].astype(F32) + three[...].astype(F32)
        )
    for flip, out in zip((1, 2, 0), outs, strict=True):
        out[...] = total[floor_ref[0] ^ flip].astype(out.dtype)


def third_sum_kernel(arrived, held, out):
    out[...] = (arrived[...].astype(F32) + held[...].astype(F32)).astype(BF16)


def expert_partial(rows, weights, scales):
    blocks, side = scales.shape[0], weights.shape[0] // scales.shape[0]
    scaled = [
        (weights[at * side : (at + 1) * side].astype(F32) * scales[at]).astype(BF16)
        for at in range(blocks)
    ]
    scaled = jnp.concatenate(scaled, axis=0)
    return jnp.dot(rows, scaled, preferred_element_type=F32).astype(BF16)


def expert_kernel(
    core_ref, rows, rows_trained, weights, weights_other, scales, scales_other, out
):
    half, wide = weights.shape
    step = pl.program_id(0)
    total = 0.0
    for core, kept, scale in (
        (core_ref[0], weights, scales),
        (1 - core_ref[0], weights_other, scales_other),
    ):
        at = pl.ds(pl.multiple_of(core * half, half), half)
        total = total + expert_partial(rows[:, at], kept, scale).astype(F32)
    chips = out.shape[0]
    count = rows.shape[0] // chips
    for chip in range(chips):
        out[chip, :count, pl.ds(pl.multiple_of(step * wide, wide), wide)] = total[
            chip * count : (chip + 1) * count
        ].astype(out.dtype)

    @pl.when(step == 0)
    def _():
        columns = wide * pl.num_programs(0)
        for chip in range(chips):
            out[chip, :count, columns:] = rows[chip * count : (chip + 1) * count, 2 * half :]
            out[chip, count:, : 2 * half] = rows_trained[...]
            out[chip, count:, 2 * half :] = jnp.zeros(
                (out.shape[1] - count, out.shape[2] - 2 * half), out.dtype
            )


def trained_kernel(device_ref, plane, depth, column_blocks, rows, *rest):
    weights, outs = rest[: 2 * depth], rest[2 * depth :]
    device = device_ref[0]
    blocks, side, _ = weights[0].shape
    floor = device // plane
    chip = device % plane // 2
    chips, count, _ = rows.shape
    for core in range(2):
        number = device % 2 ^ core
        for at in range(blocks):
            total = jnp.zeros((chips * count, side), F32)
            for flip in range(depth):
                block = (floor ^ flip) * plane * blocks + (chip * 2 + number) * blocks + at
                start = pl.multiple_of(block // column_blocks * side, side)
                part = jnp.concatenate(
                    [rows[chip ^ turn, :, pl.ds(start, side)] for turn in range(chips)], axis=0
                )
                total = total + jnp.dot(
                    part, weights[core * depth + flip][at], preferred_element_type=F32
                )
            column = pl.ds(pl.multiple_of((number * blocks + at) * side, side), side)
            for turn in range(chips):
                outs[turn][:, column] = total[turn * count : (turn + 1) * count].astype(BF16)


def mix_kernel(depth, plane_slots, floor_ref, returned, own, across, sent):
    count, columns = own.shape
    outs = own, sent.at[0], across, sent.at[1]

    def of_chips(at):
        return jnp.concatenate(
            [returned[chip, :plane_slots, at] for chip in range(returned.shape[0])], axis=0
        )

    gates = of_chips(slice(columns, None)).astype(F32)
    share = plane_slots // depth
    pieces = [gates[top : top + share] for top in range(0, gates.shape[0], share)]
    mine = []
    for flip in range(depth):
        there = floor_ref[0] ^ flip
        kept = [jnp.where(there == at % depth, piece, 0.0) for at, piece in enumerate(pieces)]
        mine.append(jnp.concatenate(kept, axis=0).astype(BF16))
    wide = 512
    for column in range(0, columns, wide):
        at = slice(column, column + wide)
        rows = of_chips(at)
        for flip, out in enumerate(outs):
            mixed = lax.dot_general(
                mine[flip], rows, (((0,), (0,)), ((), ())), preferred_element_type=F32
            )
            out[:, at] = (mixed[:count] + mixed[count : 2 * count]).astype(out.dtype)


def mix_sum_kernel(arrived, across, own, out_across, out_own):
    out_across[...] = (arrived[1].astype(F32) + across[...]).astype(BF16)
    out_own[...] = arrived[0].astype(F32) + own[...]


def combine_kernel(chip_ref, chips, side, gates_trained, near, across, *rest):
    trained, out, fresh = rest[:chips], rest[chips], rest[chips + 1]
    columns = out.shape[1]
    blocks = trained[0].shape[1] // side
    count = out.shape[0]
    fresh[...] = jnp.zeros_like(fresh)
    for turn in range(chips):
        for at in range(blocks):
            number = ((chip_ref[0] ^ turn) * blocks + at) % (columns // side)
            column = pl.ds(pl.multiple_of(number * side, side), side)
            fresh[:, column] += trained[turn][:, at * side : (at + 1) * side].astype(F32)
    wide = 512
    for column in range(0, columns, wide):
        at = slice(column, column + wide)
        both = jnp.dot(gates_trained[...], fresh[:, at].astype(BF16), preferred_element_type=F32)
        total = both[:count] + both[count:] + near[:, at] + across[:, at].astype(F32)
        out[:, at] = total.astype(out.dtype)


def local(
    learn_hidden,
    learn_cotangent,
    master,
    moment_first,
    moment_second,
    resident_weight,
    resident_scale,
    placement,
    decode_hidden,
    routing,
    gate_weight,
):
    devices = lax.axis_size("dp")
    device = lax.axis_index("dp")
    device_ref = device.astype(jnp.int32).reshape(1)
    blocks, side = master.shape[:2]
    hidden_width = learn_hidden.shape[1]
    columns = learn_cotangent.shape[1]
    row_blocks = hidden_width // side
    column_blocks = columns // side
    tokens = learn_hidden.shape[0]
    steps, step_rows, topk = routing.shape
    experts = placement.shape[0]
    capacity = min(step_rows, step_rows * topk // experts + 2)
    entries = steps * step_rows * topk
    pair_slots = steps * capacity
    slots = experts * pair_slots
    half = hidden_width // 2

    def flip(array, mask):
        return lax.ppermute(array, "dp", [(i, i ^ mask) for i in range(devices)])

    def bit(number):
        return device // 2**number % 2

    def after(array, *others):
        return lax.optimization_barrier((array, others))[0]

    def pick(array, index, axis):
        return lax.dynamic_index_in_dim(array, index, axis, keepdims=False)

    plane = 1
    while plane * blocks % column_blocks:
        plane *= 2
    depth = devices // plane
    chips = plane // 2
    floor_ref = (device // plane).astype(jnp.int32).reshape(1)
    row_count = steps * step_rows
    gate_lanes = -(-2 * row_count // 128) * 128
    smem = pl.BlockSpec(memory_space=pltpu.SMEM)
    hbm = pl.BlockSpec(memory_space=pl.ANY)

    packed, gates_trained, rows_trained = pl.pallas_call(
        lambda *refs: pack_kernel(steps, capacity, depth, *refs),
        out_shape=(
            pltpu.HBM((slots, hidden_width + gate_lanes), BF16),
            jax.ShapeDtypeStruct((2 * steps * step_rows, pair_slots), BF16),
            jax.ShapeDtypeStruct((pair_slots, hidden_width), BF16),
        ),
        in_specs=[smem] + vmem(2) + [hbm],
        out_specs=(hbm, *vmem(2)),
        scratch_shapes=[
            pltpu.VMEM((entries, hidden_width), BF16),
            pltpu.VMEM((slots, hidden_width + gate_lanes), BF16),
            pltpu.SemaphoreType.DMA,
            pltpu.SemaphoreType.DMA((4,)),
        ],
        compiler_params=PARAMS,
    )(
        *in_hbm(
            placement,
            routing.reshape(steps * step_rows, topk),
            gate_weight.reshape(steps * step_rows, topk),
            decode_hidden.reshape(entries, hidden_width),
        ),
    )
    hidden_other, cotangent_other = flip(learn_hidden, 1), flip(learn_cotangent, 1)
    same_core = [
        [z * plane + chip * 2 + core for chip in range(chips) for z in range(depth)]
        for core in range(2)
    ]
    received = lax.all_to_all(
        after(packed, hidden_other, cotangent_other).reshape(
            experts, pair_slots, hidden_width + gate_lanes
        ),
        "dp",
        split_axis=0,
        concat_axis=0,
        tiled=True,
        axis_index_groups=same_core,
    ).reshape(slots, hidden_width + gate_lanes)

    highs = devices // 16
    part = jax.ShapeDtypeStruct((highs, blocks, side, side), BF16)
    parts = pl.pallas_call(
        gradient_kernel,
        out_shape=(pltpu.HBM(part.shape, BF16),) * 8,
        in_specs=[smem] + vmem(4),
        out_specs=tuple(vmem(8)),
        scratch_shapes=[
            pltpu.VMEM((hidden_width, 2 * tokens), BF16),
            pltpu.VMEM((2 * tokens, columns), BF16),
        ],
        compiler_params=PARAMS,
    )(
        device_ref,
        *in_hbm(after(learn_hidden, packed), hidden_other, learn_cotangent, cotangent_other),
    )
    both_a, first_a, second_a, stay_a, both_b, first_b, second_b, stay_b = parts
    both_a, both_b = flip(both_a, 2), flip(both_b, 4)
    first_a, first_b = flip(first_a, 2), flip(first_b, 4)
    weights_other = flip(after(resident_weight, packed, hidden_other, cotangent_other), 1)
    scales_other = flip(resident_scale, 1)
    second_a = after(second_a, weights_other)
    second_a, second_b = pl.pallas_call(
        first_sum_kernel,
        out_shape=(pltpu.HBM(part.shape, BF16),) * 2,
        in_specs=vmem(4),
        out_specs=tuple(vmem(2)),
        compiler_params=PARAMS,
    )(both_a, *in_hbm(second_a), both_b, *in_hbm(second_b))
    sums = second_a, second_b
    second_a, second_b = flip(second_a, 4), flip(second_b, 2)

    plane_slots = depth * pair_slots
    sent_shape = (chips, plane_slots + pair_slots, columns + gate_lanes)

    def expert_sum(rows):
        wide = 512
        weight_spec = pl.BlockSpec((half, wide), lambda i, core: (0, i))
        scale_spec = pl.BlockSpec((row_blocks // 2, 1, wide), lambda i, core: (0, 0, i))
        return pl.pallas_call(
            expert_kernel,
            out_shape=pltpu.HBM(sent_shape, BF16),
            grid_spec=pltpu.PrefetchScalarGridSpec(
                num_scalar_prefetch=1,
                grid=(columns // wide,),
                in_specs=[
                    pl.BlockSpec((slots, hidden_width + gate_lanes), lambda i, core: (0, 0)),
                    pl.BlockSpec((pair_slots, hidden_width), lambda i, core: (0, 0)),
                    weight_spec,
                    weight_spec,
                    scale_spec,
                    scale_spec,
                ],
                out_specs=pl.BlockSpec(sent_shape, lambda i, core: (0, 0, 0)),
            ),
            compiler_params=PARAMS,
        )(
            bit(0).astype(jnp.int32).reshape(1),
            rows,
            rows_trained,
            resident_weight,
            weights_other,
            *(
                jnp.repeat(scales, side, axis=1)[:, None, :]
                for scales in (resident_scale, scales_other)
            ),
        )

    block_shape = (blocks, side, side)
    if highs == 2:
        expert_out = expert_sum(after(received, sums, first_a, first_b))
        parts = stay_a, first_a, second_a, stay_b, first_b, second_b
        high = (device // 8).astype(jnp.int32).reshape(1)
        piece = pl.BlockSpec((1,) + block_shape, lambda i, far: (far[0] % 2, 0, 0, 0))
        far = pl.pallas_call(
            far_sum_kernel,
            out_shape=jax.ShapeDtypeStruct(block_shape, BF16),
            grid_spec=pltpu.PrefetchScalarGridSpec(
                num_scalar_prefetch=1,
                grid=(1,),
                in_specs=[piece] * 6,
                out_specs=pl.BlockSpec(block_shape, lambda i, far: (0, 0, 0)),
            ),
            compiler_params=PARAMS,
        )(high ^ 3, *parts)
        expert_out = after(expert_out, far)
        near, across, own = pl.pallas_call(
            second_sum_kernel,
            out_shape=(
                jax.ShapeDtypeStruct(block_shape, BF16),
                jax.ShapeDtypeStruct(block_shape, F32),
                jax.ShapeDtypeStruct(block_shape, F32),
            ),
            in_specs=[smem] + vmem(6),
            out_specs=tuple(vmem(3)),
            scratch_shapes=[pltpu.VMEM((4,) + block_shape, F32)],
            compiler_params=PARAMS,
        )(after(high, far), *parts)
        far, near = flip(far, 8), flip(near, 8)
        across = pl.pallas_call(
            third_sum_kernel,
            out_shape=jax.ShapeDtypeStruct(block_shape, BF16),
            in_specs=vmem(2),
            out_specs=vmem(1)[0],
            compiler_params=PARAMS,
        )(far, across)
        gradient = [own, near, flip(across, 16)]
    else:
        expert_out = expert_sum(received)
        sums = [
            sum(piece.astype(F32) for piece in pieces)
            for pieces in ((stay_a, first_a, second_a), (stay_b, first_b, second_b))
        ]
        total = jnp.concatenate(sums, axis=0)
        number = 3
        while total.shape[0] > 1:
            split = total.reshape((-1, 2) + block_shape)
            sent = pick(split, 1 - bit(number), 1).astype(BF16)
            total = pick(split, bit(number), 1) + flip(sent, 2**number).astype(F32)
            number += 1
        gradient = [total[0]]
    new_master, fresh = pl.pallas_call(
        update_kernel,
        out_shape=(
            jax.ShapeDtypeStruct(block_shape, F32),
            jax.ShapeDtypeStruct(block_shape, BF16),
        ),
        in_specs=vmem(3 + len(gradient)),
        out_specs=tuple(vmem(2)),
        compiler_params=PARAMS,
    )(master, moment_first, moment_second, *gradient)

    same_core = [
        [z * plane + chip * 2 + core for chip in range(chips)]
        for z in range(depth)
        for core in range(2)
    ]
    returned = lax.all_to_all(
        expert_out, "dp", split_axis=0, concat_axis=0, tiled=True, axis_index_groups=same_core
    )
    rows_trained = returned[:, plane_slots:, :hidden_width]
    row_shape = (row_count, columns)
    mixed, across_rows, sent_rows = pl.pallas_call(
        lambda *refs: mix_kernel(depth, plane_slots, *refs),
        out_shape=(
            jax.ShapeDtypeStruct(row_shape, F32),
            jax.ShapeDtypeStruct(row_shape, F32),
            jax.ShapeDtypeStruct((2,) + row_shape, BF16),
        ),
        in_specs=[smem] + vmem(1),
        out_specs=tuple(vmem(3)),
        compiler_params=PARAMS,
    )(floor_ref, after(returned, fresh))
    sent_rows = flip(sent_rows, plane)

    held = {0: fresh}
    mask = depth // 2
    while mask:
        for key in list(held):
            held[key | mask] = flip(held[key], mask * plane)
        mask //= 2
    blocks_held = [held[z] for z in range(depth)]
    blocks_held += [flip(after(block, held[depth // 2]), 1) for block in blocks_held]
    chip_ref = (device % plane // 2).astype(jnp.int32).reshape(1)
    trained = pl.pallas_call(
        lambda device_ref, *refs: trained_kernel(device_ref, plane, depth, column_blocks, *refs),
        out_shape=(jax.ShapeDtypeStruct((pair_slots, 2 * blocks * side), BF16),) * chips,
        in_specs=[smem] + vmem(1 + 2 * depth),
        out_specs=tuple(vmem(chips)),
        compiler_params=PARAMS,
    )(device_ref, after(rows_trained, mixed), *blocks_held)
    across_rows, mixed_near = pl.pallas_call(
        mix_sum_kernel,
        out_shape=(
            jax.ShapeDtypeStruct(row_shape, BF16),
            jax.ShapeDtypeStruct(row_shape, F32),
        ),
        in_specs=vmem(3),
        out_specs=tuple(vmem(2)),
        compiler_params=PARAMS,
    )(after(sent_rows, trained[0]), across_rows, mixed)
    across_rows = flip(across_rows, 2 * plane)
    trained = [trained[0]] + [flip(trained[turn], 2 * turn) for turn in range(1, chips)]
    decoded = pl.pallas_call(
        lambda chip_ref, *refs: combine_kernel(chip_ref, chips, side, *refs),
        out_shape=jax.ShapeDtypeStruct((row_count, columns), BF16),
        in_specs=[smem] + vmem(3 + chips),
        out_specs=vmem(1)[0],
        scratch_shapes=[pltpu.VMEM((pair_slots, columns), F32)],
        compiler_params=PARAMS,
    )(chip_ref, gates_trained, mixed_near, across_rows, *trained)
    return (decoded.reshape(steps, step_rows, columns), new_master)


def solution(mesh):
    return jax.shard_map(
        local,
        mesh=mesh,
        in_specs=(
            P(("groups", "dp"), None),
            P(("groups", "dp"), None),
            P("dp", None, None),
            P("dp", None, None),
            P("dp", None, None),
            P("dp", None),
            P("dp", None),
            P(),
            P(None, ("groups", "dp"), None, None),
            P(None, ("groups", "dp"), None),
            P(None, ("groups", "dp"), None),
        ),
        out_specs=(P(None, ("groups", "dp"), None), P(("groups", "dp"), None, None)),
        check_vma=False,
    )
```
